128 devices in a mesh: node: 16 (over y, x), local: 8 (over z, core).
Axes of the slice: x: 4, y: 4, z: 4, core: 2. Of those that a mesh axis runs over, the one named last changes fastest.
Arguments:
- tokens: bfloat16 [2048, 3584], P(('node', 'local')), may hold values from -6 to 6
- upstream: bfloat16 [2048, 3584], P(('node', 'local')), may hold values from -6 to 6
- routes: int32 [2048, 8], P(('node', 'local')), may hold values from 0 to 47, as said below
- combine: float32 [2048, 8], P(('node', 'local')), may hold values from 0.05 to 0.3
- seq_ids: int32 [2048], P(('node', 'local')), may hold values from 0 to 255, never falling along the last dimension, each value on 1 to 16 neighbouring positions
- ratios: float32 [256], replicated, may hold values from 0.25 to 4
- w_gate: bfloat16 [48, 3584, 1024], P('node', None, 'local'), may hold values from -0.09375 to 0.09375
- w_up: bfloat16 [48, 3584, 1024], P('node', None, 'local'), may hold values from -0.09375 to 0.09375
- w_down: bfloat16 [48, 1024, 3584], P('node', 'local'), may hold values from -0.1875 to 0.1875
Outputs:
- grad_tokens: bfloat16 [2048, 3584], P(('node', 'local'))
- grad_combine: float32 [2048, 8], P(('node', 'local'))
- grad_gate: bfloat16 [48, 3584, 1024], P('node', None, 'local')
- grad_up: bfloat16 [48, 3584, 1024], P('node', None, 'local')
- grad_down: bfloat16 [48, 1024, 3584], P('node', 'local')
The draws below stay inside these ranges and needn't reach their ends.
Inputs may be any that keep to these rules, and one draw needn't show every extreme that they name: `routes`: each row names 8 distinct experts, two in each of 4 distinct node groups. The rows of one device fall into classes of 5 rows (the last class smaller) whose rows name the same node groups; different classes of a device name disjoint groups, so no node group is named by more than 5 rows of one device, and in every draw each device has a group named by exactly 5 of its rows.
All inputs are finite; a program needn't handle non-finite values.
Results may differ from the reference program's by a relative error of at most 0.015.
Values may be sent and summed in bfloat16 or wider, within the bound.
A program may use at most 192 MiB of HBM per device.

```python
import math
import jax
import jax.numpy as jnp
import numpy as np
from jax import lax

D = 3584
H = 1024
EXP_NODE = 3
TOPK = 8
GROUP_LIMIT = 4
TOK_DEV = 16
TOKENS = 2048
EXPERTS = 48
HID_DEV = 128
CAP = 5
SEQS = 256
N_NODE = 16
N_LOCAL = 8


def draw_routes(key, part):
    key = jax.random.fold_in(key, 7)
    blocks = TOKENS // TOK_DEV
    key_group, key_token, key_drop = jax.random.split(key, 3)
    group_order = jax.vmap(lambda key_item: jax.random.permutation(key_item, N_NODE))(jax.random.split(key_group, blocks))
    token_order = jax.vmap(lambda key_item: jax.random.permutation(key_item, TOK_DEV))(jax.random.split(key_token, blocks))
    member = token_order // CAP
    lanes = member[:, :, None] * GROUP_LIMIT + jnp.arange(GROUP_LIMIT, dtype=jnp.int32)[None, None, :]
    groups = jax.vmap(lambda order_row, lane_rows: order_row[lane_rows])(group_order, lanes)
    dropped = jax.random.randint(key_drop, (blocks, TOK_DEV, GROUP_LIMIT), 0, EXP_NODE)
    picks = (dropped[..., None] + 1 + jnp.arange(TOPK // GROUP_LIMIT, dtype=jnp.int32)[None, None, None, :]) % EXP_NODE
    expert_ids = groups[..., None] * EXP_NODE + picks
    return expert_ids.reshape(TOKENS, TOPK).astype(jnp.int32)


def steps_of(own_key, dims, cuts, least, top_value):
    def one(axis_at, parts):
        steps = jax.random.uniform(jax.random.fold_in(jax.random.fold_in(own_key, 6), axis_at), (parts,), jnp.float32, least / len(cuts), top_value / len(cuts))
        return jnp.repeat(jnp.exp(steps), dims[axis_at] // parts).reshape((-1,) + (1,) * (len(dims) - axis_at - 1))

    factor_of = one(*cuts[0])
    for cut in cuts[1:]:
        factor_of = factor_of * one(*cut)
    return factor_of


def profile(amount, total, limit, skew):
    loads = [(1 << 20) // math.isqrt(grade ** skew) + 1 for grade in range(2, amount + 1)]
    rest, given = total - limit - (amount - 1), [1] * (amount - 1)
    while rest > 0:
        free = [i for i in range(amount - 1) if given[i] < limit]
        mass, left = sum([loads[i] for i in free]), rest
        for i in free:
            extra = min(limit - given[i], max(1, left * loads[i] // mass), rest)
            given[i] = given[i] + extra
            rest = rest - extra
    return np.array([limit] + given)


def ragged(own_key, amount, total, reach, slope):
    if amount == 2:
        one = jax.random.randint(own_key, (), max(1, total - reach), min(reach, total - 1) + 1)
        return jnp.stack([one, total - one])
    sizes = jnp.asarray(profile(amount, total, reach, slope), jnp.int32)
    couples = (amount - 1) // 2
    donor, sink = sizes[1:1 + 2 * couples:2], sizes[2:2 + 2 * couples:2]
    room = jnp.minimum(donor - 1, reach - sink)
    shifted = jax.random.randint(jax.random.fold_in(own_key, 1), (couples,), 0, 1 << 20) % (room + 1)
    sizes = sizes.at[1:1 + 2 * couples:2].set(donor - shifted).at[2:2 + 2 * couples:2].set(sink + shifted)
    return sizes[jax.random.permutation(jax.random.fold_in(own_key, 2), amount)]


def scatter_about(own_key, extent, spread, bound, cuts=(), kind=jnp.bfloat16):
    result = spread * jax.random.normal(own_key, extent, jnp.float32)
    if cuts:
        result = result * steps_of(own_key, extent, cuts, -0.22, 0.18)
    return jnp.clip(result, -bound, bound).astype(kind)


def setup_inputs(seed: int = 0) -> dict:
    arg_keys = jax.random.split(jax.random.key(seed), 10)
    tokens = scatter_about(arg_keys[0], (TOKENS, D), 1.0, 6.0, ((0, 128),))
    upstream = scatter_about(arg_keys[1], (TOKENS, D), 1.0, 6.0, ((0, 128),))
    routes = draw_routes(jax.random.fold_in(arg_keys[9], 71), 0)
    combine = jnp.clip(0.05 + 0.25 * jax.random.uniform(arg_keys[3], (TOKENS, TOPK), jnp.float32) ** steps_of(arg_keys[3], (TOKENS, TOPK), ((0, 128),), -0.2, 0.2), 0.05, 0.3)
    seq_ids = jnp.searchsorted(jnp.cumsum(ragged(arg_keys[4], SEQS, TOKENS, TOK_DEV, 1)), jnp.arange(TOKENS), side="right").astype(jnp.int32)
    ratios = jnp.clip(jnp.exp(jax.random.uniform(arg_keys[5], (SEQS,), jnp.float32, math.log(0.25), math.log(4.0))), 0.25, 4.0)
    w_gate = scatter_about(arg_keys[6], (EXPERTS, D, H), D ** -0.5, 0.09375, ((0, 16), (2, 8)))
    w_up = scatter_about(arg_keys[7], (EXPERTS, D, H), D ** -0.5, 0.09375, ((0, 16), (2, 8)))
    w_down = scatter_about(arg_keys[8], (EXPERTS, H, D), H ** -0.5, 0.1875, ((0, 16), (1, 8)))
    return {"tokens": tokens, "upstream": upstream, "routes": routes, "combine": combine, "seq_ids": seq_ids, "ratios": ratios, "w_gate": w_gate, "w_up": w_up, "w_down": w_down}


def reference(tokens, upstream, routes, combine, seq_ids, ratios, w_gate, w_up, w_down):
    group_rows = N_NODE * N_LOCAL * CAP
    seq_weight = jnp.minimum(ratios, 1.0)[seq_ids]
    route_weight = (combine * seq_weight[:, None]).astype(jnp.bfloat16).astype(jnp.float32)
    group_of = routes // EXP_NODE

    def one_group(group_index):
        group_hit = jnp.any(group_of == group_index, axis=1)
        row_order = jnp.nonzero(group_hit, size=group_rows, fill_value=0)[0].astype(jnp.int32)
        valid_rows = (jnp.arange(group_rows, dtype=jnp.int32) < jnp.sum(group_hit.astype(jnp.int32))).astype(jnp.float32)
        group_tokens = tokens[row_order]
        group_upstream = upstream[row_order]
        chosen_routes = routes[row_order]
        chosen_weight = route_weight[row_order]
        first_expert = (group_index * EXP_NODE).astype(jnp.int32)
        gate_block = lax.dynamic_slice_in_dim(w_gate, first_expert, EXP_NODE, 0)
        up_block = lax.dynamic_slice_in_dim(w_up, first_expert, EXP_NODE, 0)
        down_block = lax.dynamic_slice_in_dim(w_down, first_expert, EXP_NODE, 0)
        partial_value = jnp.zeros((group_rows, N_LOCAL, D), jnp.float32)
        score_list = []
        grad_gate_list = []
        grad_up_list = []
        grad_down_list = []
        for expert in range(EXP_NODE):
            row_scale = jnp.sum(jnp.where(chosen_routes == first_expert + expert, chosen_weight, 0.0), axis=1) * valid_rows
            row_scale = row_scale[:, None]
            gate_pre = jnp.dot(group_tokens, gate_block[expert], preferred_element_type=jnp.float32)
            up_pre = jnp.dot(group_tokens, up_block[expert], preferred_element_type=jnp.float32)
            projected = jnp.dot(group_upstream, down_block[expert].T, preferred_element_type=jnp.float32)
            gate_sigmoid = jax.nn.sigmoid(gate_pre)
            activated = gate_pre * gate_sigmoid
            hidden = (activated * up_pre).astype(jnp.bfloat16)
            score_blocks = jnp.sum((hidden.astype(jnp.float32) * projected).reshape(group_rows, N_LOCAL, HID_DEV), axis=2)
            score_list.append(jnp.sum(score_blocks.astype(jnp.bfloat16).astype(jnp.float32), axis=1).astype(jnp.bfloat16))
            d_hidden = row_scale * projected
            d_gate = (d_hidden * up_pre * gate_sigmoid * (1.0 + gate_pre * (1.0 - gate_sigmoid))).astype(jnp.bfloat16)
            d_up = (d_hidden * activated).astype(jnp.bfloat16)
            scaled = (hidden.astype(jnp.float32) * row_scale).astype(jnp.bfloat16)
            partial_value = partial_value + jnp.einsum("rbh,dbh->rbd", d_gate.astype(jnp.float32).reshape(group_rows, N_LOCAL, HID_DEV), gate_block[expert].astype(jnp.float32).reshape(D, N_LOCAL, HID_DEV))
            partial_value = partial_value + jnp.einsum("rbh,dbh->rbd", d_up.astype(jnp.float32).reshape(group_rows, N_LOCAL, HID_DEV), up_block[expert].astype(jnp.float32).reshape(D, N_LOCAL, HID_DEV))
            grad_gate_list.append(jnp.dot(group_tokens.T, d_gate, preferred_element_type=jnp.float32).astype(jnp.bfloat16))
            grad_up_list.append(jnp.dot(group_tokens.T, d_up, preferred_element_type=jnp.float32).astype(jnp.bfloat16))
            grad_down_list.append(jnp.dot(scaled.T, group_upstream, preferred_element_type=jnp.float32).astype(jnp.bfloat16))
        contribution = jnp.sum(partial_value.astype(jnp.bfloat16).astype(jnp.float32), axis=1).astype(jnp.bfloat16)
        group_score = jnp.stack(score_list, axis=1)
        position = jnp.maximum(jnp.cumsum(group_hit.astype(jnp.int32)) - 1, 0).astype(jnp.int32)
        token_score = group_score[position]
        return contribution, row_order, token_score, jnp.stack(grad_gate_list), jnp.stack(grad_up_list), jnp.stack(grad_down_list)

    contributions, orders, token_scores, grad_gate, grad_up, grad_down = lax.map(one_group, jnp.arange(N_NODE, dtype=jnp.int32))
    grad_tokens = jnp.zeros((TOKENS, D), jnp.float32).at[orders.reshape(-1)].add(contributions.reshape(-1, D).astype(jnp.float32))
    flat_scores = jnp.transpose(token_scores, (1, 0, 2)).reshape(TOKENS, EXPERTS).astype(jnp.float32)
    grad_combine = seq_weight[:, None] * jnp.take_along_axis(flat_scores, routes, axis=1)
    return (grad_tokens.astype(jnp.bfloat16), grad_combine, grad_gate.reshape(EXPERTS, D, H), grad_up.reshape(EXPERTS, D, H), grad_down.reshape(EXPERTS, H, D))
```

```python
import jax
import jax.numpy as jnp
from jax import lax
from jax.experimental import pallas as pl
from jax.experimental.pallas import tpu as pltpu
from jax.sharding import PartitionSpec as P

MESH = pl.DeviceIdType.MESH
BF = jnp.bfloat16
F32 = jnp.float32
I32 = jnp.int32

D = 3584
DT = D + 128
PW = 1152
ROWS = 80
CA = 1792
POS = {0: 0, 1: 1, 3: 2, 2: 3}
NT = (((1,), (1,)), ((), ()))
TN = (((0,), (0,)), ((), ()))


def slot(dz, dc):
    return pl.ds((POS[dz] * 2 + dc) * ROWS, ROWS)


def inverse(q):
    return ((-(q // 4)) % 4) * 4 + (-(q % 4)) % 4


def iota(shape, dim):
    return lax.broadcasted_iota(I32, shape, dim)


def one_hot(mask):
    return jnp.where(mask, 1.0, 0.0).astype(BF)


def kernel(
    tok, ups, routes, routes_t, combine, seq_ids, ratios, wg, wu, wd,
    gt, gc, gg, gu, gd,
    amat, bmat, x3, pack_t, pack_u, pack_b, got_t, got_u, got_b, xb, ub, wall, wdn, pre, dall, scl, pb, sb,
    ra, rb, fin, x4, gw, gdn,
    wsem, ts, tr, us, ur, bs_sem, br_sem, zs, zr, rs, rr, gsem,
):
    node = lax.axis_index("node")
    loc = lax.axis_index("local")
    y, x = node // 4, node % 4
    z, c = loc // 2, loc % 2

    def xy_dev(q):
        return (((y + q // 4) % 4) * 4 + (x + q % 4) % 4, loc)

    def z_dev(dz):
        return (node, ((z + dz) % 4) * 2 + c)

    sib = (node, z * 2 + 1 - c)

    loads = []
    for e in range(3):
        loads.append(pltpu.make_async_copy(wg.at[e], wall.at[:, pl.ds(256 * e, 128)], wsem.at[3 * e]))
        loads.append(pltpu.make_async_copy(wu.at[e], wall.at[:, pl.ds(256 * e + 128, 128)], wsem.at[3 * e + 1]))
        loads.append(pltpu.make_async_copy(wd.at[e], wdn.at[pl.ds(128 * e, 128), :], wsem.at[3 * e + 2]))
    for copy in loads:
        copy.start()

    barrier = pltpu.get_barrier_semaphore()
    for q in range(1, 16):
        pl.semaphore_signal(barrier, inc=1, device_id=xy_dev(q), device_id_type=MESH)
    for peer in (z_dev(1), z_dev(3), sib):
        pl.semaphore_signal(barrier, inc=1, device_id=peer, device_id_type=MESH)

    row = iota((256, 128), 0)
    lane = iota((256, 128), 1)
    q = row >> 4
    r = row & 15
    blk = lane >> 4
    g = (((y + (q >> 2)) & 3) << 2) + ((x + (q & 3)) & 3)
    lo = 3 * g
    hit = jnp.zeros((256, 128), F32)
    for k in range(8):
        rk = routes_t[k : k + 1, :]
        hit = jnp.where((rk >= lo) & (rk < lo + 3), 1.0, hit)
    ui = iota((128, 128), 0)
    uj = iota((128, 128), 1)
    before = one_hot(((ui >> 4) == (uj >> 4)) & ((ui & 15) < (uj & 15)))
    place = jnp.dot(hit.astype(BF), before, preferred_element_type=F32).astype(I32)
    want = jnp.where(blk < 3, jnp.where(r < 15, r - 5 * blk, -1), jnp.where(r == 15, blk - 3, -1))
    amat[...] = one_hot((hit > 0.5) & (place == want) & (want >= 0) & (want < 5))

    hot = seq_ids[...] == iota((16, 256), 1)
    seq_w = jnp.sum(jnp.where(hot, jnp.minimum(ratios[...], 1.0), 0.0), axis=1, keepdims=True)
    rw = (combine[...] * seq_w).astype(BF).astype(F32)
    lane16 = iota((16, 128), 1)
    weights = []
    for half in range(2):
        acc = jnp.zeros((16, 128), F32)
        for k in range(8):
            acc = acc + jnp.where(routes[:, k : k + 1] == lane16 - 64 * half, rw[:, k : k + 1], 0.0)
        weights.append(acc.astype(BF))

    def spread(src):
        x3[...] = jnp.zeros((128, PW), BF)
        for j in range(3):
            x3[pl.ds(16 * j, 16), :] = src[:, PW * j : PW * (j + 1)]
        for j in range(5):
            x3[pl.ds(48 + 16 * j, 16), pl.ds(128 * j, 128)] = src[:, 3 * PW : D]

    spread(tok)
    for j in range(5):
        x3[pl.ds(48 + 16 * j, 16), pl.ds(128 * (5 + j // 2), 128)] = weights[j % 2]
    pack_t[...] = jnp.dot(amat[...], x3[...], preferred_element_type=F32).astype(BF)

    pl.semaphore_wait(barrier, 18)

    def xy_copies(src, dst, ssem, rsem):
        return [
            pltpu.make_async_remote_copy(
                src_ref=src.at[pl.ds(16 * k, 16), :],
                dst_ref=dst.at[pl.ds(16 * inverse(k), 16), :],
                send_sem=ssem.at[k],
                recv_sem=rsem.at[inverse(k)],
                device_id=xy_dev(k),
                device_id_type=MESH,
            )
            for k in range(1, 16)
        ]

    sent_t = xy_copies(pack_t, got_t, ts, tr)
    for copy in sent_t:
        copy.start()
    got_t[pl.ds(0, 16), :] = pack_t[pl.ds(0, 16), :]

    spread(ups)
    pack_u[...] = jnp.dot(amat[...], x3[...], preferred_element_type=F32).astype(BF)
    sent_u = xy_copies(pack_u, got_u, us, ur)
    for copy in sent_u:
        copy.start()
    got_u[pl.ds(0, 16), :] = pack_u[pl.ds(0, 16), :]

    brow = iota((4 * ROWS, 256), 0)
    part = jnp.where(brow >= 80, 1, 0) + jnp.where(brow >= 160, 1, 0) + jnp.where(brow >= 240, 1, 0)
    rem = brow - 80 * part
    bq = (rem * 205) >> 10
    bs = rem - 5 * bq
    bmat[...] = one_hot(iota((4 * ROWS, 256), 1) == bq * 16 + jnp.where(part < 3, 5 * part + bs, 15))

    drow = iota((ROWS, 128), 0)
    dlane = iota((ROWS, 128), 1)
    ds_ = drow - 5 * ((drow * 205) >> 10)

    def unpack(got, dst):
        dense = jnp.dot(bmat[...], got[...], preferred_element_type=F32)
        for j in range(3):
            dst[pl.ds(0, ROWS), pl.ds(PW * j, PW)] = dense[ROWS * j : ROWS * (j + 1), :].astype(BF)
        last = dense[3 * ROWS : 4 * ROWS, :]
        tail = jnp.zeros((ROWS, 128), F32)
        for j in range(5):
            tail = jnp.where(ds_ == j, last[:, 128 * j : 128 * (j + 1)], tail)
        dst[pl.ds(0, ROWS), pl.ds(3 * PW, 128)] = tail.astype(BF)
        return last

    def remote(k, src, dst, device, ssem, rsem):
        return pltpu.make_async_remote_copy(
            src_ref=src, dst_ref=dst, send_sem=ssem.at[k], recv_sem=rsem.at[k],
            device_id=device, device_id_type=MESH,
        )

    def gather_copy(k, buf, src, dst, device):
        return remote(k, buf.at[slot(*src), :], buf.at[slot(*dst), :], device, zs, zr)

    tp = gather_copy(0, xb, (0, 0), (3, 0), z_dev(1))
    tm = gather_copy(1, xb, (0, 0), (1, 0), z_dev(3))
    tf = gather_copy(2, xb, (3, 0), (2, 0), z_dev(1))
    t_sib = {dz: gather_copy(3 + dz, xb, (dz, 0), (dz, 1), sib) for dz in range(4)}
    up = gather_copy(7, ub, (0, 0), (3, 0), z_dev(1))
    um = gather_copy(8, ub, (0, 0), (1, 0), z_dev(3))
    uf = gather_copy(9, ub, (1, 0), (2, 0), z_dev(3))
    u_sib = {dz: gather_copy(10 + dz, ub, (dz, 0), (dz, 1), sib) for dz in range(4)}

    for copy in sent_t:
        copy.wait_recv()
    last = unpack(got_t, xb)
    picked = jnp.zeros((ROWS, 128), F32)
    for j in range(5):
        mine = (ds_ == j) & ((dlane >> 6) == j % 2)
        picked = jnp.where(mine, last[:, 128 * (5 + j // 2) : 128 * (6 + j // 2)], picked)
    take = one_hot(((ui & 63) == 3 * node + uj) & (uj < 3))
    xb[pl.ds(0, ROWS), pl.ds(D, 128)] = jnp.dot(picked.astype(BF), take, preferred_element_type=F32).astype(BF)
    tp.start()
    tm.start()
    t_sib[0].start()

    for copy in sent_u:
        copy.wait_recv()
    unpack(got_u, ub)
    up.start()
    um.start()
    u_sib[0].start()

    def compute(r0, m):
        rows = pl.ds(r0, m)
        for e in range(3):
            pre[pl.ds(0, m), pl.ds(256 * e, 256)] = jnp.dot(
                xb[rows, pl.ds(0, D)], wall[:, pl.ds(256 * e, 256)], preferred_element_type=F32
            )
        proj_all = lax.dot_general(ub[rows, :], wdn[...], NT, preferred_element_type=F32)
        score = jnp.zeros((m, 128), F32)
        lanes = iota((m, 128), 1)
        for e in range(3):
            gate = pre[pl.ds(0, m), pl.ds(256 * e, 128)]
            upv = pre[pl.ds(0, m), pl.ds(256 * e + 128, 128)]
            proj = proj_all[:, 128 * e : 128 * (e + 1)]
            scale = xb[rows, pl.ds(D, 128)][:, e : e + 1].astype(F32)
            sig = jax.nn.sigmoid(gate)
            act = gate * sig
            hidden = (act * upv).astype(BF).astype(F32)
            score = jnp.where(lanes == e, jnp.sum(hidden * proj, axis=1, keepdims=True), score)
            dh = scale * proj
            dall[rows, pl.ds(256 * e, 128)] = (dh * upv * sig * (1.0 + gate * (1.0 - sig))).astype(BF)
            dall[rows, pl.ds(256 * e + 128, 128)] = (dh * act).astype(BF)
            scl[rows, pl.ds(128 * e, 128)] = (hidden * scale).astype(BF)
        pb[rows, pl.ds(D, 128)] = score.astype(BF)

        @pl.loop(0, 7)
        def _(i):
            cols = pl.ds(pl.multiple_of(i * 512, 512), 512)
            pb[rows, cols] = lax.dot_general(
                dall[rows, :], wall[cols, :], NT, preferred_element_type=F32
            ).astype(BF)

    p_sib = {
        dz: remote(dz, pb.at[slot(dz, 1), :], sb.at[pl.ds(POS[dz] * ROWS, ROWS), :], sib, rs, rr)
        for dz in range(4)
    }

    def pair_sum(dz):
        p_sib[dz].wait_recv()
        pb[slot(dz, 0), :] = (
            pb[slot(dz, 0), :].astype(F32) + sb[pl.ds(POS[dz] * ROWS, ROWS), :].astype(F32)
        ).astype(BF)

    for copy in loads:
        copy.wait()
    t_sib[0].wait_recv()
    u_sib[0].wait_recv()
    compute(0, 160)
    p_sib[0].start()

    tp.wait_recv()
    tf.start()
    t_sib[3].start()
    tm.wait_recv()
    t_sib[1].start()
    um.wait_recv()
    uf.start()
    u_sib[1].start()
    up.wait_recv()
    u_sib[3].start()
    for dz in (1, 3):
        t_sib[dz].wait_recv()
        u_sib[dz].wait_recv()
    compute(160, 320)
    p_sib[1].start()
    p_sib[3].start()

    tf.wait_recv()
    t_sib[2].start()
    uf.wait_recv()
    u_sib[2].start()
    t_sib[2].wait_recv()
    u_sib[2].wait_recv()
    compute(480, 160)
    p_sib[2].start()

    first = pl.ds(0, CA)
    second = pl.ds(CA, DT - CA)
    q2a = remote(4, pb.at[slot(2, 0), first], ra, z_dev(1), rs, rr)
    q2b = remote(5, pb.at[slot(2, 0), second], rb, z_dev(3), rs, rr)
    r1a = remote(6, pb.at[slot(1, 0), first], fin.at[0, :, first], z_dev(1), rs, rr)
    r1b = remote(7, pb.at[slot(1, 0), second], fin.at[0, :, second], z_dev(1), rs, rr)
    r3a = remote(8, pb.at[slot(3, 0), first], fin.at[1, :, first], z_dev(3), rs, rr)
    r3b = remote(9, pb.at[slot(3, 0), second], fin.at[1, :, second], z_dev(3), rs, rr)

    pair_sum(2)
    q2a.start()
    q2b.start()
    pair_sum(1)
    r1b.start()
    pair_sum(3)
    r3a.start()

    def weight_grads(lo_, hi_):
        @pl.loop(lo_, hi_)
        def _(i):
            cols = pl.ds(pl.multiple_of(i * 512, 512), 512)
            gw[cols, :] = lax.dot_general(xb[:, cols], dall[...], TN, preferred_element_type=F32).astype(BF)

    def down_grads(lo_, hi_):
        @pl.loop(lo_, hi_)
        def _(i):
            cols = pl.ds(pl.multiple_of(i * 512, 512), 512)
            gdn[:, cols] = lax.dot_general(scl[...], ub[:, cols], TN, preferred_element_type=F32).astype(BF)

    weight_grads(0, 7)
    q2a.wait_recv()
    pb[slot(1, 0), first] = (pb[slot(1, 0), first].astype(F32) + ra[...].astype(F32)).astype(BF)
    r1a.start()
    q2b.wait_recv()
    pb[slot(3, 0), second] = (pb[slot(3, 0), second].astype(F32) + rb[...].astype(F32)).astype(BF)
    r3b.start()

    outs = []
    for e in range(3):
        outs.append(pltpu.make_async_copy(gw.at[:, pl.ds(256 * e, 128)], gg.at[e], gsem.at[e]))
        outs.append(pltpu.make_async_copy(gw.at[:, pl.ds(256 * e + 128, 128)], gu.at[e], gsem.at[3 + e]))
    for copy in outs:
        copy.start()
    down_grads(0, 7)
    downs = [
        pltpu.make_async_copy(gdn.at[pl.ds(128 * e, 128), :], gd.at[e], gsem.at[6 + e]) for e in range(3)
    ]
    for copy in downs:
        copy.start()

    pair_sum(0)
    for copy in (r1b, r3a, r1a, r3b):
        copy.wait_recv()
    total = pb[slot(0, 0), :].astype(F32) + fin[0].astype(F32) + fin[1].astype(F32)
    x4[...] = jnp.zeros((384, PW), BF)
    for j in range(3):
        x4[pl.ds(ROWS * j, ROWS), :] = total[:, PW * j : PW * (j + 1)].astype(BF)
    tail = total[:, 3 * PW : D]
    for j in range(5):
        x4[pl.ds(3 * ROWS, ROWS), pl.ds(128 * j, 128)] = jnp.where(ds_ == j, tail, 0.0).astype(BF)
    repeat = one_hot((ui == (uj & 7)) & (ui < 3))
    score = jnp.dot(total[:, D:DT].astype(BF), repeat, preferred_element_type=F32)
    x4[pl.ds(3 * ROWS, ROWS), pl.ds(640, 128)] = jnp.where((dlane >> 3) == ds_, score, 0.0).astype(BF)
    crow = iota((256, 384), 0)
    clane = iota((256, 384), 1)
    cpart = jnp.where(clane >= 80, 1, 0) + jnp.where(clane >= 160, 1, 0) + jnp.where(clane >= 240, 1, 0)
    crem = clane - 80 * cpart
    cq = (crem * 205) >> 10
    cs = crem - 5 * cq
    cmat = one_hot((crow == cq * 16 + jnp.where(cpart < 3, 5 * cpart + cs, 15)) & (clane < 320))
    pack_b[...] = jnp.dot(cmat, x4[...], preferred_element_type=F32).astype(BF)
    sent_b = xy_copies(pack_b, got_b, bs_sem, br_sem)
    for copy in sent_b:
        copy.start()
    got_b[pl.ds(0, 16), :] = pack_b[pl.ds(0, 16), :]
    for copy in sent_b:
        copy.wait_recv()

    summed = lax.dot_general(amat[...], got_b[...], TN, preferred_element_type=F32)
    for j in range(3):
        gt[:, pl.ds(PW * j, PW)] = summed[16 * j : 16 * (j + 1), :].astype(BF)
    tail = jnp.zeros((16, 128), F32)
    for j in range(5):
        tail = tail + summed[48 + 16 * j : 64 + 16 * j, 128 * j : 128 * (j + 1)]
    gt[:, pl.ds(3 * PW, 128)] = tail.astype(BF)

    third = uj - 3 * ((uj * 171) >> 9)
    token_score = jnp.zeros((16, 128), F32)
    for j in range(5):
        pick = one_hot(ui == 8 * j + third)
        wide = jnp.dot(got_b[:, pl.ds(640, 128)], pick, preferred_element_type=F32)
        wide = jnp.where((lane >= lo) & (lane < lo + 3), wide, 0.0).astype(BF)
        share = lax.dot_general(amat[...], wide, TN, preferred_element_type=F32)
        token_score = token_score + share[48 + 16 * j : 64 + 16 * j, :]
    result = jnp.zeros((16, 128), F32)
    for k in range(8):
        value = jnp.sum(jnp.where(routes[:, k : k + 1] == lane16, token_score, 0.0), axis=1, keepdims=True)
        result = jnp.where(lane16 == k, value * seq_w, result)
    gc[...] = result[:, :8]

    for copy in sent_t + sent_u + sent_b:
        copy.wait_send()
    for copy in (tp, tm, tf, up, um, uf, q2a, q2b, r1a, r1b, r3a, r3b):
        copy.wait_send()
    for dz in range(4):
        t_sib[dz].wait_send()
        u_sib[dz].wait_send()
        p_sib[dz].wait_send()
    for copy in outs + downs:
        copy.wait()


def local(tokens, upstream, routes, combine, seq_ids, ratios, w_gate, w_up, w_down):
    vmem = pl.BlockSpec(memory_space=pltpu.VMEM)
    hbm = pl.BlockSpec(memory_space=pl.ANY)
    shape = jax.ShapeDtypeStruct
    dma = pltpu.SemaphoreType.DMA
    return pl.pallas_call(
        kernel,
        out_shape=(
            shape((16, D), BF),
            shape((16, 8), F32),
            shape((3, D, 128), BF),
            shape((3, D, 128), BF),
            shape((3, 128, D), BF),
        ),
        in_specs=[vmem] * 7 + [hbm] * 3,
        out_specs=(vmem, vmem, hbm, hbm, hbm),
        scratch_shapes=[
            pltpu.VMEM((256, 128), BF),
            pltpu.VMEM((320, 256), BF),
            pltpu.VMEM((128, PW), BF),
            pltpu.VMEM((256, PW), BF),
            pltpu.VMEM((256, PW), BF),
            pltpu.VMEM((256, PW), BF),
            pltpu.VMEM((256, PW), BF),
            pltpu.VMEM((256, PW), BF),
            pltpu.VMEM((256, PW), BF),
            pltpu.VMEM((640, DT), BF),
            pltpu.VMEM((640, D), BF),
            pltpu.VMEM((D, 768), BF),
            pltpu.VMEM((384, D), BF),
            pltpu.VMEM((320, 768), F32),
            pltpu.VMEM((640, 768), BF),
            pltpu.VMEM((640, 384), BF),
            pltpu.VMEM((640, DT), BF),
            pltpu.VMEM((320, DT), BF),
            pltpu.VMEM((ROWS, CA), BF),
            pltpu.VMEM((ROWS, DT - CA), BF),
            pltpu.VMEM((2, ROWS, DT), BF),
            pltpu.VMEM((384, PW), BF),
            pltpu.VMEM((D, 768), BF),
            pltpu.VMEM((384, D), BF),
            dma((9,)),
            dma((16,)), dma((16,)), dma((16,)), dma((16,)), dma((16,)), dma((16,)),
            dma((14,)), dma((14,)), dma((10,)), dma((10,)), dma((9,)),
        ],
        compiler_params=pltpu.CompilerParams(
            collective_id=0, has_side_effects=True, vmem_limit_bytes=58 << 20
        ),
        name="moe_grad",
    )(
        tokens, upstream, routes, jnp.tile(routes.T, (1, 8)), combine,
        seq_ids[:, None], ratios[None, :], w_gate, w_up, w_down,
    )


def solution(mesh):
    rows = P(("node", "local"), None)
    return jax.shard_map(
        local,
        mesh=mesh,
        in_specs=(
            rows, rows, rows, rows, P(("node", "local")), P(),
            P("node", None, "local"), P("node", None, "local"), P("node", "local", None),
        ),
        out_specs=(rows, rows, P("node", None, "local"), P("node", None, "local"), P("node", "local", None)),
        check_vma=False,
    )
```

```python
import jax
import jax.numpy as jnp
from jax import lax
from jax.experimental import pallas as pl
from jax.experimental.pallas import tpu as pltpu
from jax.sharding import PartitionSpec as P

MESH = pl.DeviceIdType.MESH
BF = jnp.bfloat16
F32 = jnp.float32
I32 = jnp.int32

D = 3584
DT = D + 128
PW = 1152
ROWS = 80
CA = 1792
POS = {0: 0, 1: 1, 3: 2, 2: 3}
NT = (((1,), (1,)), ((), ()))
TN = (((0,), (0,)), ((), ()))


def slot(dz, dc):
    return pl.ds((POS[dz] * 2 + dc) * ROWS, ROWS)


def inverse(q):
    return ((-(q // 4)) % 4) * 4 + (-(q % 4)) % 4


def iota(shape, dim):
    return lax.broadcasted_iota(I32, shape, dim)


def one_hot(mask):
    return jnp.where(mask, 1.0, 0.0).astype(BF)


def seq_weight(seq_ids, ratios):
    hot = jnp.where(iota((256, 16), 0) == seq_ids[...], 1.0, 0.0)
    clipped = jnp.broadcast_to(jnp.minimum(ratios[...], 1.0), (8, 256))
    return jnp.dot(clipped, hot, precision=lax.Precision.HIGHEST, preferred_element_type=F32)


def kernel(
    tok, ups, routes_t, combine_t, seq_ids, ratios, wg, wu, wd,
    amat, got_b, gg, gu, gd,
    bmat, x3, pack_t, pack_u, pack_b, got_t, got_u, xb, ub, wall, wdn, pre, dall, scl, pb, sb,
    ra, rb, fin, x4,
    wsem, ts, tr, us, ur, bs_sem, br_sem, zs, zr, rs, rr,
):
    node = lax.axis_index("node")
    loc = lax.axis_index("local")
    y, x = node // 4, node % 4
    z, c = loc // 2, loc % 2

    def xy_dev(q):
        return (((y + q // 4) % 4) * 4 + (x + q % 4) % 4, loc)

    def z_dev(dz):
        return (node, ((z + dz) % 4) * 2 + c)

    sib = (node, z * 2 + 1 - c)

    loads = []
    for e in range(3):
        loads.append(pltpu.make_async_copy(wg.at[e], wall.at[:, pl.ds(256 * e, 128)], wsem.at[3 * e]))
        loads.append(pltpu.make_async_copy(wu.at[e], wall.at[:, pl.ds(256 * e + 128, 128)], wsem.at[3 * e + 1]))
        loads.append(pltpu.make_async_copy(wd.at[e], wdn.at[pl.ds(128 * e, 128), :], wsem.at[3 * e + 2]))
    for copy in loads:
        copy.start()

    barrier = pltpu.get_barrier_semaphore()
    for q in range(1, 16):
        pl.semaphore_signal(barrier, inc=1, device_id=xy_dev(q), device_id_type=MESH)
    for peer in (z_dev(1), z_dev(3), sib):
        pl.semaphore_signal(barrier, inc=1, device_id=peer, device_id_type=MESH)

    seq_w = seq_weight(seq_ids, ratios)
    rw = (combine_t[...] * seq_w).astype(BF).astype(F32)
    tiled = jnp.dot(
        routes_t[...].astype(F32).astype(BF),
        one_hot((iota((16, 128), 1) & 15) == iota((16, 128), 0)),
        preferred_element_type=F32,
    ).astype(I32)

    row = iota((256, 128), 0)
    lane = iota((256, 128), 1)
    q = row >> 4
    r = row & 15
    blk = lane >> 4
    g = (((y + (q >> 2)) & 3) << 2) + ((x + (q & 3)) & 3)
    lo = 3 * g
    hit = jnp.zeros((256, 128), F32)
    for k in range(8):
        rk = tiled[k : k + 1, :]
        hit = jnp.where((rk >= lo) & (rk < lo + 3), 1.0, hit)
    ui = iota((128, 128), 0)
    uj = iota((128, 128), 1)
    before = one_hot(((ui >> 4) == (uj >> 4)) & ((ui & 15) < (uj & 15)))
    place = jnp.dot(hit.astype(BF), before, preferred_element_type=F32).astype(I32)
    want = jnp.where(blk < 3, jnp.where(r < 15, r - 5 * blk, -1), jnp.where(r == 15, blk - 3, -1))
    amat[...] = one_hot((hit > 0.5) & (place == want) & (want >= 0) & (want < 5))

    expert = iota((128, 16), 0)
    same = one_hot(ui == uj)
    weights = []
    for half in range(2):
        acc = jnp.zeros((128, 16), F32)
        for k in range(8):
            acc = acc + jnp.where(routes_t[k : k + 1, :] == expert - 64 * half, rw[k : k + 1, :], 0.0)
        weights.append(
            lax.dot_general(acc.astype(BF), same, TN, preferred_element_type=F32).astype(BF)
        )

    def spread(src):
        x3[...] = jnp.zeros((128, PW), BF)
        for j in range(3):
            x3[pl.ds(16 * j, 16), :] = src[:, PW * j : PW * (j + 1)]
        for j in range(5):
            x3[pl.ds(48 + 16 * j, 16), pl.ds(128 * j, 128)] = src[:, 3 * PW : D]

    spread(tok)
    for j in range(5):
        x3[pl.ds(48 + 16 * j, 16), pl.ds(128 * (5 + j // 2), 128)] = weights[j % 2]
    pack_t[...] = jnp.dot(amat[...], x3[...], preferred_element_type=F32).astype(BF)

    pl.semaphore_wait(barrier, 18)

    def xy_copies(src, dst, ssem, rsem):
        return [
            pltpu.make_async_remote_copy(
                src_ref=src.at[pl.ds(16 * k, 16), :],
                dst_ref=dst.at[pl.ds(16 * inverse(k), 16), :],
                send_sem=ssem.at[k],
                recv_sem=rsem.at[inverse(k)],
                device_id=xy_dev(k),
                device_id_type=MESH,
            )
            for k in range(1, 16)
        ]

    sent_t = xy_copies(pack_t, got_t, ts, tr)
    for copy in sent_t:
        copy.start()
    got_t[pl.ds(0, 16), :] = pack_t[pl.ds(0, 16), :]

    spread(ups)
    pack_u[...] = jnp.dot(amat[...], x3[...], preferred_element_type=F32).astype(BF)
    sent_u = xy_copies(pack_u, got_u, us, ur)
    for copy in sent_u:
        copy.start()
    got_u[pl.ds(0, 16), :] = pack_u[pl.ds(0, 16), :]

    brow = iota((4 * ROWS, 256), 0)
    part = jnp.where(brow >= 80, 1, 0) + jnp.where(brow >= 160, 1, 0) + jnp.where(brow >= 240, 1, 0)
    rem = brow - 80 * part
    bq = (rem * 205) >> 10
    bs = rem - 5 * bq
    bmat[...] = one_hot(iota((4 * ROWS, 256), 1) == bq * 16 + jnp.where(part < 3, 5 * part + bs, 15))

    drow = iota((ROWS, 128), 0)
    dlane = iota((ROWS, 128), 1)
    ds_ = drow - 5 * ((drow * 205) >> 10)

    def unpack(got, dst):
        dense = jnp.dot(bmat[...], got[...], preferred_element_type=F32)
        for j in range(3):
            dst[pl.ds(0, ROWS), pl.ds(PW * j, PW)] = dense[ROWS * j : ROWS * (j + 1), :].astype(BF)
        last = dense[3 * ROWS : 4 * ROWS, :]
        tail = jnp.zeros((ROWS, 128), F32)
        for j in range(5):
            tail = jnp.where(ds_ == j, last[:, 128 * j : 128 * (j + 1)], tail)
        dst[pl.ds(0, ROWS), pl.ds(3 * PW, 128)] = tail.astype(BF)
        return last

    def remote(k, src, dst, device, ssem, rsem):
        return pltpu.make_async_remote_copy(
            src_ref=src, dst_ref=dst, send_sem=ssem.at[k], recv_sem=rsem.at[k],
            device_id=device, device_id_type=MESH,
        )

    def gather_copy(k, buf, src, dst, device):
        return remote(k, buf.at[slot(*src), :], buf.at[slot(*dst), :], device, zs, zr)

    tp = gather_copy(0, xb, (0, 0), (3, 0), z_dev(1))
    tm = gather_copy(1, xb, (0, 0), (1, 0), z_dev(3))
    tf = gather_copy(2, xb, (3, 0), (2, 0), z_dev(1))
    t_sib = {dz: gather_copy(3 + dz, xb, (dz, 0), (dz, 1), sib) for dz in range(4)}
    up = gather_copy(7, ub, (0, 0), (3, 0), z_dev(1))
    um = gather_copy(8, ub, (0, 0), (1, 0), z_dev(3))
    uf = gather_copy(9, ub, (1, 0), (2, 0), z_dev(3))
    u_sib = {dz: gather_copy(10 + dz, ub, (dz, 0), (dz, 1), sib) for dz in range(4)}

    for copy in sent_t:
        copy.wait_recv()
    last = unpack(got_t, xb)
    picked = jnp.zeros((ROWS, 128), F32)
    for j in range(5):
        mine = (ds_ == j) & ((dlane >> 6) == j % 2)
        picked = jnp.where(mine, last[:, 128 * (5 + j // 2) : 128 * (6 + j // 2)], picked)
    take = one_hot(((ui & 63) == 3 * node + uj) & (uj < 3))
    xb[pl.ds(0, ROWS), pl.ds(D, 128)] = jnp.dot(picked.astype(BF), take, preferred_element_type=F32).astype(BF)
    tp.start()
    tm.start()
    t_sib[0].start()

    for copy in sent_u:
        copy.wait_recv()
    unpack(got_u, ub)
    up.start()
    um.start()
    u_sib[0].start()

    def compute(r0, m):
        rows = pl.ds(r0, m)
        for e in range(3):
            pre[pl.ds(0, m), pl.ds(256 * e, 256)] = jnp.dot(
                xb[rows, pl.ds(0, D)], wall[:, pl.ds(256 * e, 256)], preferred_element_type=F32
            )
        proj_all = lax.dot_general(ub[rows, :], wdn[...], NT, preferred_element_type=F32)
        score = jnp.zeros((m, 128), F32)
        lanes = iota((m, 128), 1)
        for e in range(3):
            gate = pre[pl.ds(0, m), pl.ds(256 * e, 128)]
            upv = pre[pl.ds(0, m), pl.ds(256 * e + 128, 128)]
            proj = proj_all[:, 128 * e : 128 * (e + 1)]
            scale = xb[rows, pl.ds(D, 128)][:, e : e + 1].astype(F32)
            sig = jax.nn.sigmoid(gate)
            act = gate * sig
            hidden = (act * upv).astype(BF).astype(F32)
            score = jnp.where(lanes == e, jnp.sum(hidden * proj, axis=1, keepdims=True), score)
            dh = scale * proj
            dall[rows, pl.ds(256 * e, 128)] = (dh * upv * sig * (1.0 + gate * (1.0 - sig))).astype(BF)
            dall[rows, pl.ds(256 * e + 128, 128)] = (dh * act).astype(BF)
            scl[rows, pl.ds(128 * e, 128)] = (hidden * scale).astype(BF)
        pb[rows, pl.ds(D, 128)] = score.astype(BF)

        @pl.loop(0, 7)
        def _(i):
            cols = pl.ds(pl.multiple_of(i * 512, 512), 512)
            pb[rows, cols] = lax.dot_general(
                dall[rows, :], wall[cols, :], NT, preferred_element_type=F32
            ).astype(BF)

    p_sib = {
        dz: remote(dz, pb.at[slot(dz, 1), :], sb.at[pl.ds(POS[dz] * ROWS, ROWS), :], sib, rs, rr)
        for dz in range(4)
    }

    def pair_sum(dz):
        p_sib[dz].wait_recv()
        pb[slot(dz, 0), :] = (
            pb[slot(dz, 0), :].astype(F32) + sb[pl.ds(POS[dz] * ROWS, ROWS), :].astype(F32)
        ).astype(BF)

    for copy in loads:
        copy.wait()
    t_sib[0].wait_recv()
    u_sib[0].wait_recv()
    compute(0, 160)
    p_sib[0].start()

    tp.wait_recv()
    tf.start()
    t_sib[3].start()
    tm.wait_recv()
    t_sib[1].start()
    um.wait_recv()
    uf.start()
    u_sib[1].start()
    up.wait_recv()
    u_sib[3].start()
    for dz in (1, 3):
        t_sib[dz].wait_recv()
        u_sib[dz].wait_recv()
    compute(160, 320)
    p_sib[1].start()
    p_sib[3].start()

    tf.wait_recv()
    t_sib[2].start()
    uf.wait_recv()
    u_sib[2].start()
    t_sib[2].wait_recv()
    u_sib[2].wait_recv()
    compute(480, 160)
    p_sib[2].start()

    first = pl.ds(0, CA)
    second = pl.ds(CA, DT - CA)
    q2a = remote(4, pb.at[slot(2, 0), first], ra, z_dev(1), rs, rr)
    q2b = remote(5, pb.at[slot(2, 0), second], rb, z_dev(3), rs, rr)
    r1a = remote(6, pb.at[slot(1, 0), first], fin.at[0, :, first], z_dev(1), rs, rr)
    r1b = remote(7, pb.at[slot(1, 0), second], fin.at[0, :, second], z_dev(1), rs, rr)
    r3a = remote(8, pb.at[slot(3, 0), first], fin.at[1, :, first], z_dev(3), rs, rr)
    r3b = remote(9, pb.at[slot(3, 0), second], fin.at[1, :, second], z_dev(3), rs, rr)

    pair_sum(2)
    q2a.start()
    q2b.start()
    pair_sum(1)
    r1b.start()
    pair_sum(3)
    r3a.start()

    def weight_grads(lo_, hi_):
        @pl.loop(lo_, hi_)
        def _(i):
            cols = pl.ds(pl.multiple_of(i * 512, 512), 512)
            grads = lax.dot_general(xb[:, cols], dall[...], TN, preferred_element_type=F32).astype(BF)
            for e in range(3):
                gg[e, cols, :] = grads[:, 256 * e : 256 * e + 128]
                gu[e, cols, :] = grads[:, 256 * e + 128 : 256 * (e + 1)]

    def down_grads(lo_, hi_):
        @pl.loop(lo_, hi_)
        def _(i):
            cols = pl.ds(pl.multiple_of(i * 512, 512), 512)
            grads = lax.dot_general(scl[...], ub[:, cols], TN, preferred_element_type=F32).astype(BF)
            for e in range(3):
                gd[e, :, cols] = grads[128 * e : 128 * (e + 1), :]

    weight_grads(0, 7)
    q2a.wait_recv()
    pb[slot(1, 0), first] = (pb[slot(1, 0), first].astype(F32) + ra[...].astype(F32)).astype(BF)
    r1a.start()
    q2b.wait_recv()
    pb[slot(3, 0), second] = (pb[slot(3, 0), second].astype(F32) + rb[...].astype(F32)).astype(BF)
    r3b.start()

    down_grads(0, 7)

    pair_sum(0)
    for copy in (r1b, r3a, r1a, r3b):
        copy.wait_recv()
    total = pb[slot(0, 0), :].astype(F32) + fin[0].astype(F32) + fin[1].astype(F32)
    x4[...] = jnp.zeros((384, PW), BF)
    for j in range(3):
        x4[pl.ds(ROWS * j, ROWS), :] = total[:, PW * j : PW * (j + 1)].astype(BF)
    tail = total[:, 3 * PW : D]
    for j in range(5):
        x4[pl.ds(3 * ROWS, ROWS), pl.ds(128 * j, 128)] = jnp.where(ds_ == j, tail, 0.0).astype(BF)
    repeat = one_hot((ui == (uj & 7)) & (ui < 3))
    score = jnp.dot(total[:, D:DT].astype(BF), repeat, preferred_element_type=F32)
    x4[pl.ds(3 * ROWS, ROWS), pl.ds(640, 128)] = jnp.where((dlane >> 3) == ds_, score, 0.0).astype(BF)
    crow = iota((256, 384), 0)
    clane = iota((256, 384), 1)
    cpart = jnp.where(clane >= 80, 1, 0) + jnp.where(clane >= 160, 1, 0) + jnp.where(clane >= 240, 1, 0)
    crem = clane - 80 * cpart
    cq = (crem * 205) >> 10
    cs = crem - 5 * cq
    cmat = one_hot((crow == cq * 16 + jnp.where(cpart < 3, 5 * cpart + cs, 15)) & (clane < 320))
    pack_b[...] = jnp.dot(cmat, x4[...], preferred_element_type=F32).astype(BF)
    sent_b = xy_copies(pack_b, got_b, bs_sem, br_sem)
    for copy in sent_b:
        copy.start()
    got_b[pl.ds(0, 16), :] = pack_b[pl.ds(0, 16), :]
    for copy in sent_b:
        copy.wait_recv()

    for copy in sent_t + sent_u + sent_b:
        copy.wait_send()
    for copy in (tp, tm, tf, up, um, uf, q2a, q2b, r1a, r1b, r3a, r3b):
        copy.wait_send()
    for dz in range(4):
        t_sib[dz].wait_send()
        u_sib[dz].wait_send()
        p_sib[dz].wait_send()


def finish(amat, got_b, routes_t, seq_ids, ratios, gg_in, gu_in, gd_in, gt, gc, gg, gu, gd, sems):
    copies = []
    for k, (src, dst) in enumerate(((gg_in, gg), (gu_in, gu), (gd_in, gd))):
        for e in range(3):
            copies.append(pltpu.make_async_copy(src.at[e], dst.at[e], sems.at[3 * k + e]))
    for copy in copies:
        copy.start()
    node = lax.axis_index("node")
    y, x = node // 4, node % 4
    row = iota((256, 128), 0)
    lane = iota((256, 128), 1)
    q = row >> 4
    lo = 3 * ((((y + (q >> 2)) & 3) << 2) + ((x + (q & 3)) & 3))
    ui = iota((128, 128), 0)
    uj = iota((128, 128), 1)
    seq_w = seq_weight(seq_ids, ratios)
    summed = lax.dot_general(amat[...], got_b[...], TN, preferred_element_type=F32)
    for j in range(3):
        gt[:, pl.ds(PW * j, PW)] = summed[16 * j : 16 * (j + 1), :].astype(BF)
    tail = jnp.zeros((16, 128), F32)
    for j in range(5):
        tail = tail + summed[48 + 16 * j : 64 + 16 * j, 128 * j : 128 * (j + 1)]
    gt[:, pl.ds(3 * PW, 128)] = tail.astype(BF)

    third = uj - 3 * ((uj * 171) >> 9)
    token_score = jnp.zeros((16, 128), F32)
    for j in range(5):
        pick = one_hot(ui == 8 * j + third)
        wide = jnp.dot(got_b[:, pl.ds(640, 128)], pick, preferred_element_type=F32)
        wide = jnp.where((lane >= lo) & (lane < lo + 3), wide, 0.0).astype(BF)
        share = lax.dot_general(amat[...], wide, TN, preferred_element_type=F32)
        token_score = token_score + share[48 + 16 * j : 64 + 16 * j, :]
    eye = one_hot(iota((16, 16), 0) == iota((16, 16), 1))
    scores = lax.dot_general(token_score.astype(BF), eye, TN, preferred_element_type=F32)
    expert = iota((128, 16), 0)
    for k in range(8):
        value = jnp.sum(jnp.where(routes_t[k : k + 1, :] == expert, scores, 0.0), axis=0, keepdims=True)
        gc[pl.ds(k, 1), :] = value * seq_w[k : k + 1, :]
    for copy in copies:
        copy.wait()


def local(tokens, upstream, routes, combine, seq_ids, ratios, w_gate, w_up, w_down):
    vmem = pl.BlockSpec(memory_space=pltpu.VMEM)
    hbm = pl.BlockSpec(memory_space=pl.ANY)
    shape = jax.ShapeDtypeStruct
    dma = pltpu.SemaphoreType.DMA
    routes_t, combine_t, seq_ids, ratios = routes.T, combine.T, seq_ids[None, :], ratios[None, :]
    amat, got_b, *grads = pl.pallas_call(
        kernel,
        out_shape=(
            pltpu.VMEM((256, 128), BF),
            pltpu.VMEM((256, PW), BF),
            pltpu.VMEM((3, D, 128), BF),
            pltpu.VMEM((3, D, 128), BF),
            pltpu.VMEM((3, 128, D), BF),
        ),
        in_specs=[vmem] * 6 + [hbm] * 3,
        out_specs=(vmem,) * 5,
        scratch_shapes=[
            pltpu.VMEM((320, 256), BF),
            pltpu.VMEM((128, PW), BF),
            pltpu.VMEM((256, PW), BF),
            pltpu.VMEM((256, PW), BF),
            pltpu.VMEM((256, PW), BF),
            pltpu.VMEM((256, PW), BF),
            pltpu.VMEM((256, PW), BF),
            pltpu.VMEM((640, DT), BF),
            pltpu.VMEM((640, D), BF),
            pltpu.VMEM((D, 768), BF),
            pltpu.VMEM((384, D), BF),
            pltpu.VMEM((320, 768), F32),
            pltpu.VMEM((640, 768), BF),
            pltpu.VMEM((640, 384), BF),
            pltpu.VMEM((640, DT), BF),
            pltpu.VMEM((320, DT), BF),
            pltpu.VMEM((ROWS, CA), BF),
            pltpu.VMEM((ROWS, DT - CA), BF),
            pltpu.VMEM((2, ROWS, DT), BF),
            pltpu.VMEM((384, PW), BF),
            dma((9,)),
            dma((16,)), dma((16,)), dma((16,)), dma((16,)), dma((16,)), dma((16,)),
            dma((14,)), dma((14,)), dma((10,)), dma((10,)),
        ],
        compiler_params=pltpu.CompilerParams(
            collective_id=0, has_side_effects=True, vmem_limit_bytes=46 << 20
        ),
        name="moe_grad",
    )(tokens, upstream, routes_t, combine_t, seq_ids, ratios, w_gate, w_up, w_down)
    gt, gc, gg, gu, gd = pl.pallas_call(
        finish,
        out_shape=(
            shape((16, D), BF),
            shape((8, 16), F32),
            shape((3, D, 128), BF),
            shape((3, D, 128), BF),
            shape((3, 128, D), BF),
        ),
        in_specs=[vmem] * 8,
        out_specs=(vmem, vmem, hbm, hbm, hbm),
        scratch_shapes=[dma((9,))],
        compiler_params=pltpu.CompilerParams(vmem_limit_bytes=16 << 20),
        name="moe_finish",
    )(amat, got_b, routes_t, seq_ids, ratios, *grads)
    return gt, gc.T, gg, gu, gd


def solution(mesh):
    rows = P(("node", "local"), None)
    return jax.shard_map(
        local,
        mesh=mesh,
        in_specs=(
            rows, rows, rows, rows, P(("node", "local")), P(),
            P("node", None, "local"), P("node", None, "local"), P("node", "local", None),
        ),
        out_specs=(rows, rows, P("node", None, "local"), P("node", None, "local"), P("node", "local", None)),
        check_vma=False,
    )
```

```python
import jax
import jax.numpy as jnp
from jax import lax
from jax.experimental import pallas as pl
from jax.experimental.pallas import tpu as pltpu
from jax.sharding import PartitionSpec as P

MESH = pl.DeviceIdType.MESH
BF = jnp.bfloat16
F32 = jnp.float32
I32 = jnp.int32

D = 3584
DT = D + 128
PW = 1152
ROWS = 80
POS = {0: 0, 1: 1, 3: 2, 2: 3}
NEAR = (1, 3, 4, 12, 2, 5, 7, 8, 13, 15, 6, 9, 11, 14, 10)
NT = (((1,), (1,)), ((), ()))
TN = (((0,), (0,)), ((), ()))


def slot(dz, dc):
    return pl.ds((POS[dz] * 2 + dc) * ROWS, ROWS)


def inverse(q):
    return ((-(q // 4)) % 4) * 4 + (-(q % 4)) % 4


def iota(shape, dim):
    return lax.broadcasted_iota(I32, shape, dim)


def one_hot(mask):
    return jnp.where(mask, 1.0, 0.0).astype(BF)


def seq_weight(seq_ids, ratios):
    hot = jnp.where(iota((256, 16), 0) == seq_ids[...], 1.0, 0.0)
    clipped = jnp.broadcast_to(jnp.minimum(ratios[...], 1.0), (8, 256))
    return jnp.dot(clipped, hot, precision=lax.Precision.HIGHEST, preferred_element_type=F32)


def route_matrix(tiled, y, x):
    row = iota((256, 128), 0)
    lane = iota((256, 128), 1)
    r = row & 15
    blk = lane >> 4
    lo = first_expert(row, y, x)
    hit = jnp.zeros((256, 128), F32)
    for k in range(8):
        rk = tiled[k : k + 1, :]
        hit = jnp.where((rk >= lo) & (rk < lo + 3), 1.0, hit)
    ui = iota((128, 128), 0)
    uj = iota((128, 128), 1)
    before = one_hot(((ui >> 4) == (uj >> 4)) & ((ui & 15) < (uj & 15)))
    place = jnp.dot(hit.astype(BF), before, preferred_element_type=F32).astype(I32)
    want = jnp.where(blk < 3, jnp.where(r < 15, r - 5 * blk, -1), jnp.where(r == 15, blk - 3, -1))
    return one_hot((hit > 0.5) & (place == want) & (want >= 0) & (want < 5))


def first_expert(row, y, x):
    q = row >> 4
    return 3 * ((((y + (q >> 2)) & 3) << 2) + ((x + (q & 3)) & 3))


def token_sums(amat, got, y, x):
    row = iota((256, 128), 0)
    lane = iota((256, 128), 1)
    lo = first_expert(row, y, x)
    summed = lax.dot_general(amat[...], got[...], TN, preferred_element_type=F32)
    parts = [summed[16 * j : 16 * (j + 1), :] for j in range(3)]
    tail = jnp.zeros((16, 128), F32)
    for j in range(5):
        tail = tail + summed[48 + 16 * j : 64 + 16 * j, 128 * j : 128 * (j + 1)]
    ui = iota((128, 128), 0)
    uj = iota((128, 128), 1)
    third = uj - 3 * ((uj * 171) >> 9)
    score = jnp.zeros((16, 128), F32)
    for j in range(5):
        pick = one_hot(ui == 8 * j + third)
        wide = jnp.dot(got[:, pl.ds(640, 128)], pick, preferred_element_type=F32)
        wide = jnp.where((lane >= lo) & (lane < lo + 3), wide, 0.0).astype(BF)
        share = lax.dot_general(amat[...], wide, TN, preferred_element_type=F32)
        score = score + share[48 + 16 * j : 64 + 16 * j, :]
    return parts, tail, score


def kernel(
    tok, ups, routes_t, combine_t, seq_ids, ratios, wg, wu, wd,
    amat, got_b, far, gg, gu, gd,
    amat2, bmat, cmat, x3, info, tok2, ups2, info2, far_out,
    pack_t, pack_u, pack_t2, pack_u2, pack_b, pack_b2, got_t, got_u, got_t2, got_u2, got_b2,
    xb, ub, wall, wdn, pre, dall, scl, pb, sb, fin, x4,
    wsem, xs, xr, zs, zr,
):
    node = lax.axis_index("node")
    loc = lax.axis_index("local")
    y, x = node // 4, node % 4
    z, c = loc // 2, loc % 2

    def xy_dev(q):
        return (((y + q // 4) % 4) * 4 + (x + q % 4) % 4, loc)

    def z_dev(dz):
        return (node, ((z + dz) % 4) * 2 + c)

    sib = (node, z * 2 + 1 - c)

    loads = []
    for e in range(3):
        loads.append(pltpu.make_async_copy(wg.at[e], wall.at[:, pl.ds(256 * e, 128)], wsem.at[3 * e]))
        loads.append(pltpu.make_async_copy(wu.at[e], wall.at[:, pl.ds(256 * e + 128, 128)], wsem.at[3 * e + 1]))
        loads.append(pltpu.make_async_copy(wd.at[e], wdn.at[pl.ds(128 * e, 128), :], wsem.at[3 * e + 2]))

    barrier = pltpu.get_barrier_semaphore()
    for q in range(1, 16):
        pl.semaphore_signal(barrier, inc=1, device_id=xy_dev(q), device_id_type=MESH)
    for peer in (z_dev(1), z_dev(2), z_dev(3), sib):
        pl.semaphore_signal(barrier, inc=1, device_id=peer, device_id_type=MESH)

    started = []

    def start(copy):
        copy.start()
        started.append(copy)

    def remote(k, src, dst, device):
        return pltpu.make_async_remote_copy(
            src_ref=src, dst_ref=dst, send_sem=zs.at[k], recv_sem=zr.at[k],
            device_id=device, device_id_type=MESH,
        )

    def xy_send(k, src, dst):
        copies = [
            pltpu.make_async_remote_copy(
                src_ref=src.at[pl.ds(16 * q, 16), :],
                dst_ref=dst.at[pl.ds(16 * inverse(q), 16), :],
                send_sem=xs.at[k, q],
                recv_sem=xr.at[k, inverse(q)],
                device_id=xy_dev(q),
                device_id_type=MESH,
            )
            for q in NEAR
        ]
        for copy in copies:
            start(copy)
        dst[pl.ds(0, 16), :] = src[pl.ds(0, 16), :]
        return copies

    def arrive(copies):
        for copy in copies:
            copy.wait_recv()

    ui = iota((128, 128), 0)
    uj = iota((128, 128), 1)
    seq_w = seq_weight(seq_ids, ratios)
    rw = (combine_t[...] * seq_w).astype(BF).astype(F32)
    tiled = jnp.dot(
        routes_t[...].astype(F32).astype(BF),
        one_hot((iota((16, 128), 1) & 15) == iota((16, 128), 0)),
        preferred_element_type=F32,
    )
    info[:, pl.ds(256, 128)] = jnp.concatenate([tiled, jnp.zeros((8, 128), F32)], axis=0).astype(BF)
    expert = iota((128, 16), 0)
    same = one_hot(ui == uj)
    for half in range(2):
        acc = jnp.zeros((128, 16), F32)
        for k in range(8):
            acc = acc + jnp.where(routes_t[k : k + 1, :] == expert - 64 * half, rw[k : k + 1, :], 0.0)
        info[:, pl.ds(128 * half, 128)] = lax.dot_general(
            acc.astype(BF), same, TN, preferred_element_type=F32
        ).astype(BF)

    def pack_in(src, mat, dst, notes=None):
        x3[...] = jnp.zeros((128, PW), BF)
        for j in range(3):
            x3[pl.ds(16 * j, 16), :] = src[:, PW * j : PW * (j + 1)]
        for j in range(5):
            x3[pl.ds(48 + 16 * j, 16), pl.ds(128 * j, 128)] = src[:, 3 * PW : D]
        if notes is not None:
            for j in range(5):
                x3[pl.ds(48 + 16 * j, 16), pl.ds(128 * (5 + j // 2), 128)] = notes[:, pl.ds(128 * (j % 2), 128)]
        dst[...] = jnp.dot(mat[...], x3[...], preferred_element_type=F32).astype(BF)

    amat[...] = route_matrix(tiled.astype(I32), y, x)
    pack_in(tok, amat, pack_t, info)

    raw_i = remote(0, info, info2, z_dev(2))
    raw_t = remote(1, tok, tok2, z_dev(2))
    raw_u = remote(2, ups, ups2, z_dev(2))

    pl.semaphore_wait(barrier, 19)
    sent_t = xy_send(0, pack_t, got_t)
    start(raw_i)
    start(raw_t)
    pack_in(ups, amat, pack_u)
    sent_u = xy_send(1, pack_u, got_u)
    start(raw_u)
    for copy in loads:
        copy.start()

    brow = iota((4 * ROWS, 256), 0)
    part = jnp.where(brow >= 80, 1, 0) + jnp.where(brow >= 160, 1, 0) + jnp.where(brow >= 240, 1, 0)
    rem = brow - 80 * part
    bq = (rem * 205) >> 10
    bs = rem - 5 * bq
    bmat[...] = one_hot(iota((4 * ROWS, 256), 1) == bq * 16 + jnp.where(part < 3, 5 * part + bs, 15))
    drow = iota((ROWS, 128), 0)
    dlane = iota((ROWS, 128), 1)
    ds_ = drow - 5 * ((drow * 205) >> 10)
    take = one_hot(((ui & 63) == 3 * node + uj) & (uj < 3))

    raw_i.wait_recv()
    amat2[...] = route_matrix(info2[:, pl.ds(256, 128)].astype(F32).astype(I32), y, x)
    raw_t.wait_recv()
    pack_in(tok2, amat2, pack_t2, info2)

    def unpack(got, dst, place, notes):
        dense = jnp.dot(bmat[...], got[...], preferred_element_type=F32)
        for j in range(3):
            dst[place, pl.ds(PW * j, PW)] = dense[ROWS * j : ROWS * (j + 1), :].astype(BF)
        last = dense[3 * ROWS : 4 * ROWS, :]
        tail = jnp.zeros((ROWS, 128), F32)
        for j in range(5):
            tail = jnp.where(ds_ == j, last[:, 128 * j : 128 * (j + 1)], tail)
        dst[place, pl.ds(3 * PW, 128)] = tail.astype(BF)
        if notes:
            picked = jnp.zeros((ROWS, 128), F32)
            for j in range(5):
                mine = (ds_ == j) & ((dlane >> 6) == j % 2)
                picked = jnp.where(mine, last[:, 128 * (5 + j // 2) : 128 * (6 + j // 2)], picked)
            dst[place, pl.ds(D, 128)] = jnp.dot(picked.astype(BF), take, preferred_element_type=F32).astype(BF)

    def gather_copy(k, buf, src, dst, device):
        return remote(k, buf.at[slot(*src), :], buf.at[slot(*dst), :], device)

    tp = gather_copy(3, xb, (0, 0), (3, 0), z_dev(1))
    tm = gather_copy(4, xb, (0, 0), (1, 0), z_dev(3))
    up = gather_copy(5, ub, (0, 0), (3, 0), z_dev(1))
    um = gather_copy(6, ub, (0, 0), (1, 0), z_dev(3))
    t_sib = {dz: gather_copy(7 + dz, xb, (dz, 0), (dz, 1), sib) for dz in range(4)}
    u_sib = {dz: gather_copy(11 + dz, ub, (dz, 0), (dz, 1), sib) for dz in range(4)}

    arrive(sent_t)
    sent_t2 = xy_send(2, pack_t2, got_t2)
    unpack(got_t, xb, slot(0, 0), True)
    start(tp)
    start(tm)
    start(t_sib[0])

    raw_u.wait_recv()
    pack_in(ups2, amat2, pack_u2)
    arrive(sent_u)
    sent_u2 = xy_send(3, pack_u2, got_u2)
    unpack(got_u, ub, slot(0, 0), False)
    start(up)
    start(um)
    start(u_sib[0])

    def gate_up(r0, m):
        rows = pl.ds(r0, m)
        for e in range(3):
            pre[rows, pl.ds(256 * e, 256)] = jnp.dot(
                xb[rows, pl.ds(0, D)], wall[:, pl.ds(256 * e, 256)], preferred_element_type=F32
            )

    def backward(r0, m):
        rows = pl.ds(r0, m)
        proj_all = lax.dot_general(ub[rows, :], wdn[...], NT, preferred_element_type=F32)
        score = jnp.zeros((m, 128), F32)
        lanes = iota((m, 128), 1)
        for e in range(3):
            gate = pre[rows, pl.ds(256 * e, 128)]
            upv = pre[rows, pl.ds(256 * e + 128, 128)]
            proj = proj_all[:, 128 * e : 128 * (e + 1)]
            scale = xb[rows, pl.ds(D, 128)][:, e : e + 1].astype(F32)
            sig = jax.nn.sigmoid(gate)
            act = gate * sig
            hidden = (act * upv).astype(BF).astype(F32)
            score = jnp.where(lanes == e, jnp.sum(hidden * proj, axis=1, keepdims=True), score)
            dh = scale * proj
            dall[rows, pl.ds(256 * e, 128)] = (dh * upv * sig * (1.0 + gate * (1.0 - sig))).astype(BF)
            dall[rows, pl.ds(256 * e + 128, 128)] = (dh * act).astype(BF)
            scl[rows, pl.ds(128 * e, 128)] = (hidden * scale).astype(BF)
        pb[rows, pl.ds(D, 128)] = score.astype(BF)

        @pl.loop(0, 7)
        def _(i):
            cols = pl.ds(pl.multiple_of(i * 512, 512), 512)
            pb[rows, cols] = lax.dot_general(
                dall[rows, :], wall[cols, :], NT, preferred_element_type=F32
            ).astype(BF)

    p_sib = {
        dz: remote(15 + dz, pb.at[slot(dz, 1), :], sb.at[pl.ds(POS[dz] * ROWS, ROWS), :], sib)
        for dz in range(4)
    }

    def pair_sum(dz):
        p_sib[dz].wait_recv()
        return pb[slot(dz, 0), :].astype(F32) + sb[pl.ds(POS[dz] * ROWS, ROWS), :].astype(F32)

    crow = iota((256, 384), 0)
    clane = iota((256, 384), 1)
    cpart = jnp.where(clane >= 80, 1, 0) + jnp.where(clane >= 160, 1, 0) + jnp.where(clane >= 240, 1, 0)
    crem = clane - 80 * cpart
    cq = (crem * 205) >> 10
    cs = crem - 5 * cq
    cmat[...] = one_hot((crow == cq * 16 + jnp.where(cpart < 3, 5 * cpart + cs, 15)) & (clane < 320))
    x4[...] = jnp.zeros((384, PW), BF)
    repeat = one_hot((ui == (uj & 7)) & (ui < 3))

    def pack_out(total, dst):
        for j in range(3):
            x4[pl.ds(ROWS * j, ROWS), :] = total[:, PW * j : PW * (j + 1)].astype(BF)
        tail = total[:, 3 * PW : D]
        for j in range(5):
            x4[pl.ds(3 * ROWS, ROWS), pl.ds(128 * j, 128)] = jnp.where(ds_ == j, tail, 0.0).astype(BF)
        score = jnp.dot(total[:, D:DT].astype(BF), repeat, preferred_element_type=F32)
        x4[pl.ds(3 * ROWS, ROWS), pl.ds(640, 128)] = jnp.where((dlane >> 3) == ds_, score, 0.0).astype(BF)
        dst[...] = jnp.dot(cmat[...], x4[...], preferred_element_type=F32).astype(BF)

    for copy in loads:
        copy.wait()
    t_sib[0].wait_recv()
    gate_up(0, 160)
    u_sib[0].wait_recv()
    backward(0, 160)
    start(p_sib[0])

    tp.wait_recv()
    start(t_sib[3])
    tm.wait_recv()
    start(t_sib[1])
    arrive(sent_t2)
    unpack(got_t2, xb, slot(2, 0), True)
    start(t_sib[2])
    t_sib[1].wait_recv()
    t_sib[3].wait_recv()
    gate_up(160, 320)
    t_sib[2].wait_recv()
    gate_up(480, 160)
    arrive(sent_u2)
    unpack(got_u2, ub, slot(2, 0), False)
    start(u_sib[2])
    um.wait_recv()
    start(u_sib[1])
    up.wait_recv()
    start(u_sib[3])
    u_sib[2].wait_recv()
    backward(480, 160)
    start(p_sib[2])
    u_sib[1].wait_recv()
    backward(160, 160)
    start(p_sib[1])
    pack_out(pair_sum(2), pack_b2)
    sent_b2 = xy_send(4, pack_b2, got_b2)
    u_sib[3].wait_recv()
    backward(320, 160)
    start(p_sib[3])
    r1 = remote(19, pb.at[slot(1, 0), :], fin.at[0], z_dev(1))
    r3 = remote(20, pb.at[slot(3, 0), :], fin.at[1], z_dev(3))
    pb[slot(1, 0), :] = pair_sum(1).astype(BF)
    start(r1)
    pb[slot(3, 0), :] = pair_sum(3).astype(BF)
    start(r3)

    def weight_grads(first, last):
        @pl.loop(first, last)
        def _(i):
            cols = pl.ds(pl.multiple_of(i * 512, 512), 512)
            grads = lax.dot_general(xb[:, cols], dall[...], TN, preferred_element_type=F32).astype(BF)
            for e in range(3):
                gg[e, cols, :] = grads[:, 256 * e : 256 * e + 128]
                gu[e, cols, :] = grads[:, 256 * e + 128 : 256 * (e + 1)]

    def down_grads(first, last):
        @pl.loop(first, last)
        def _(i):
            cols = pl.ds(pl.multiple_of(i * 512, 512), 512)
            grads = lax.dot_general(scl[...], ub[:, cols], TN, preferred_element_type=F32).astype(BF)
            for e in range(3):
                gd[e, :, cols] = grads[128 * e : 128 * (e + 1), :]

    weight_grads(0, 4)
    arrive(sent_b2)
    parts, tail, score = token_sums(amat2, got_b2, y, x)
    for j in range(3):
        far_out[:, pl.ds(PW * j, PW)] = parts[j].astype(BF)
    far_out[:, pl.ds(3 * PW, 128)] = tail.astype(BF)
    far_out[:, pl.ds(D, 128)] = score.astype(BF)
    raw_b = remote(21, far_out, far, z_dev(2))
    start(raw_b)
    weight_grads(4, 7)

    total = pair_sum(0)
    r1.wait_recv()
    total = total + fin[0].astype(F32)
    r3.wait_recv()
    pack_out(total + fin[1].astype(F32), pack_b)
    sent_b = xy_send(5, pack_b, got_b)
    down_grads(0, 7)
    raw_b.wait_recv()
    arrive(sent_b)
    for copy in started:
        copy.wait_send()


def finish(amat, got_b, far, routes_t, seq_ids, ratios, gg_in, gu_in, gd_in, gt, gc, gg, gu, gd, sems):
    copies = []
    for k, (src, dst) in enumerate(((gg_in, gg), (gu_in, gu), (gd_in, gd))):
        for e in range(3):
            copies.append(pltpu.make_async_copy(src.at[e], dst.at[e], sems.at[3 * k + e]))
    for copy in copies:
        copy.start()
    node = lax.axis_index("node")
    seq_w = seq_weight(seq_ids, ratios)
    parts, tail, score = token_sums(amat, got_b, node // 4, node % 4)
    for j in range(3):
        gt[:, pl.ds(PW * j, PW)] = (parts[j] + far[:, pl.ds(PW * j, PW)].astype(F32)).astype(BF)
    gt[:, pl.ds(3 * PW, 128)] = (tail + far[:, pl.ds(3 * PW, 128)].astype(F32)).astype(BF)
    score = score + far[:, pl.ds(D, 128)].astype(F32)
    eye = one_hot(iota((16, 16), 0) == iota((16, 16), 1))
    scores = lax.dot_general(score.astype(BF), eye, TN, preferred_element_type=F32)
    expert = iota((128, 16), 0)
    for k in range(8):
        value = jnp.sum(jnp.where(routes_t[k : k + 1, :] == expert, scores, 0.0), axis=0, keepdims=True)
        gc[pl.ds(k, 1), :] = value * seq_w[k : k + 1, :]
    for copy in copies:
        copy.wait()


def local(tokens, upstream, routes, combine, seq_ids, ratios, w_gate, w_up, w_down):
    vmem = pl.BlockSpec(memory_space=pltpu.VMEM)
    hbm = pl.BlockSpec(memory_space=pl.ANY)
    shape = jax.ShapeDtypeStruct
    dma = pltpu.SemaphoreType.DMA
    routes_t, combine_t, seq_ids, ratios = routes.T, combine.T, seq_ids[None, :], ratios[None, :]
    amat, got_b, far, *grads = pl.pallas_call(
        kernel,
        out_shape=(
            pltpu.VMEM((256, 128), BF),
            pltpu.VMEM((256, PW), BF),
            pltpu.VMEM((16, DT), BF),
            pltpu.VMEM((3, D, 128), BF),
            pltpu.VMEM((3, D, 128), BF),
            pltpu.VMEM((3, 128, D), BF),
        ),
        in_specs=[vmem] * 6 + [hbm] * 3,
        out_specs=(vmem,) * 6,
        scratch_shapes=[
            pltpu.VMEM((256, 128), BF),
            pltpu.VMEM((320, 256), BF),
            pltpu.VMEM((256, 384), BF),
            pltpu.VMEM((128, PW), BF),
            pltpu.VMEM((16, 384), BF),
            pltpu.VMEM((16, D), BF),
            pltpu.VMEM((16, D), BF),
            pltpu.VMEM((16, 384), BF),
            pltpu.VMEM((16, DT), BF),
        ]
        + [pltpu.VMEM((256, PW), BF)] * 11
        + [
            pltpu.VMEM((640, DT), BF),
            pltpu.VMEM((640, D), BF),
            pltpu.VMEM((D, 768), BF),
            pltpu.VMEM((384, D), BF),
            pltpu.VMEM((640, 768), F32),
            pltpu.VMEM((640, 768), BF),
            pltpu.VMEM((640, 384), BF),
            pltpu.VMEM((640, DT), BF),
            pltpu.VMEM((320, DT), BF),
            pltpu.VMEM((2, ROWS, DT), BF),
            pltpu.VMEM((384, PW), BF),
            dma((9,)), dma((6, 16)), dma((6, 16)), dma((22,)), dma((22,)),
        ],
        compiler_params=pltpu.CompilerParams(
            collective_id=0, has_side_effects=True, vmem_limit_bytes=46 << 20
        ),
        name="moe_grad",
    )(tokens, upstream, routes_t, combine_t, seq_ids, ratios, w_gate, w_up, w_down)
    gt, gc, gg, gu, gd = pl.pallas_call(
        finish,
        out_shape=(
            shape((16, D), BF),
            shape((8, 16), F32),
            shape((3, D, 128), BF),
            shape((3, D, 128), BF),
            shape((3, 128, D), BF),
        ),
        in_specs=[vmem] * 9,
        out_specs=(vmem, vmem, hbm, hbm, hbm),
        scratch_shapes=[dma((9,))],
        compiler_params=pltpu.CompilerParams(vmem_limit_bytes=16 << 20),
        name="moe_finish",
    )(amat, got_b, far, routes_t, seq_ids, ratios, *grads)
    return gt, gc.T, gg, gu, gd


def solution(mesh):
    rows = P(("node", "local"), None)
    return jax.shard_map(
        local,
        mesh=mesh,
        in_specs=(
            rows, rows, rows, rows, P(("node", "local")), P(),
            P("node", None, "local"), P("node", None, "local"), P("node", "local", None),
        ),
        out_specs=(rows, rows, P("node", None, "local"), P("node", None, "local"), P("node", "local", None)),
        check_vma=False,
    )
```

```python
import jax
import jax.numpy as jnp
from jax import lax
from jax.experimental import pallas as pl
from jax.experimental.pallas import tpu as pltpu
from jax.sharding import PartitionSpec as P

MESH = pl.DeviceIdType.MESH
BF = jnp.bfloat16
F32 = jnp.float32
I32 = jnp.int32

D = 3584
DT = D + 128
PW = 1152
ROWS = 80
POS = {0: 0, 1: 1, 3: 2, 2: 3}
NEAR = (1, 3, 4, 12, 2, 5, 7, 8, 13, 15, 6, 9, 11, 14, 10)
PIECES = ((0, 640), (640, 512))
NT = (((1,), (1,)), ((), ()))
TN = (((0,), (0,)), ((), ()))


def slot(dz, dc):
    return pl.ds((POS[dz] * 2 + dc) * ROWS, ROWS)


def dense_slices(p):
    first, width = PIECES[p]
    return [pl.ds(PW * j + first, width) for j in range(3)] + [pl.ds(3 * PW + 128 * p, 128)]


def inverse(q):
    return ((-(q // 4)) % 4) * 4 + (-(q % 4)) % 4


def iota(shape, dim):
    return lax.broadcasted_iota(I32, shape, dim)


def one_hot(mask):
    return jnp.where(mask, 1.0, 0.0).astype(BF)


def seq_weight(seq_ids, ratios):
    hot = jnp.where(iota((256, 16), 0) == seq_ids[...], 1.0, 0.0)
    clipped = jnp.broadcast_to(jnp.minimum(ratios[...], 1.0), (8, 256))
    return jnp.dot(clipped, hot, precision=lax.Precision.HIGHEST, preferred_element_type=F32)


def route_matrix(tiled, y, x):
    row = iota((256, 128), 0)
    lane = iota((256, 128), 1)
    r = row & 15
    blk = lane >> 4
    lo = first_expert(row, y, x)
    hit = jnp.zeros((256, 128), F32)
    for k in range(8):
        rk = tiled[k : k + 1, :]
        hit = jnp.where((rk >= lo) & (rk < lo + 3), 1.0, hit)
    ui = iota((128, 128), 0)
    uj = iota((128, 128), 1)
    before = one_hot(((ui >> 4) == (uj >> 4)) & ((ui & 15) < (uj & 15)))
    place = jnp.dot(hit.astype(BF), before, preferred_element_type=F32).astype(I32)
    want = jnp.where(blk < 3, jnp.where(r < 15, r - 5 * blk, -1), jnp.where(r == 15, blk - 3, -1))
    return one_hot((hit > 0.5) & (place == want) & (want >= 0) & (want < 5))


def first_expert(row, y, x):
    q = row >> 4
    return 3 * ((((y + (q >> 2)) & 3) << 2) + ((x + (q & 3)) & 3))


def token_sums(amat, got, y, x):
    row = iota((256, 128), 0)
    lane = iota((256, 128), 1)
    lo = first_expert(row, y, x)
    summed = lax.dot_general(amat[...], got[...], TN, preferred_element_type=F32)
    parts = [summed[16 * j : 16 * (j + 1), :] for j in range(3)]
    tail = jnp.zeros((16, 128), F32)
    for j in range(5):
        tail = tail + summed[48 + 16 * j : 64 + 16 * j, 128 * j : 128 * (j + 1)]
    ui = iota((128, 128), 0)
    uj = iota((128, 128), 1)
    third = uj - 3 * ((uj * 171) >> 9)
    score = jnp.zeros((16, 128), F32)
    for j in range(5):
        pick = one_hot(ui == 8 * j + third)
        wide = jnp.dot(got[:, pl.ds(640, 128)], pick, preferred_element_type=F32)
        wide = jnp.where((lane >= lo) & (lane < lo + 3), wide, 0.0).astype(BF)
        share = lax.dot_general(amat[...], wide, TN, preferred_element_type=F32)
        score = score + share[48 + 16 * j : 64 + 16 * j, :]
    return parts, tail, score


def kernel(
    tok, ups, routes_t, combine_t, seq_ids, ratios, wg, wu, wd,
    amat, got_b, far, gg, gu, gd,
    amat2, bmat, cmat, x3, info, tok2, ups2, info2, far_out,
    pack_t, pack_u, pack_t2, pack_u2, pack_b, pack_b2, got_t, got_u, got_t2, got_u2, got_b2,
    xb, ub, wall, wdn, pre, dall, scl, pb, sb, fin, x4,
    wsem, xs, xr, zs, zr,
):
    node = lax.axis_index("node")
    loc = lax.axis_index("local")
    y, x = node // 4, node % 4
    z, c = loc // 2, loc % 2

    def xy_dev(q):
        return (((y + q // 4) % 4) * 4 + (x + q % 4) % 4, loc)

    def z_dev(dz):
        return (node, ((z + dz) % 4) * 2 + c)

    sib = (node, z * 2 + 1 - c)

    loads = []
    for e in range(3):
        loads.append(pltpu.make_async_copy(wg.at[e], wall.at[:, pl.ds(256 * e, 128)], wsem.at[3 * e]))
        loads.append(pltpu.make_async_copy(wu.at[e], wall.at[:, pl.ds(256 * e + 128, 128)], wsem.at[3 * e + 1]))
        loads.append(pltpu.make_async_copy(wd.at[e], wdn.at[pl.ds(128 * e, 128), :], wsem.at[3 * e + 2]))

    barrier = pltpu.get_barrier_semaphore()
    for q in range(1, 16):
        pl.semaphore_signal(barrier, inc=1, device_id=xy_dev(q), device_id_type=MESH)
    for peer in (z_dev(1), z_dev(2), z_dev(3), sib):
        pl.semaphore_signal(barrier, inc=1, device_id=peer, device_id_type=MESH)

    started = []

    def start(copy):
        copy.start()
        started.append(copy)

    used = []

    def remote(src, dst, device):
        k = len(used)
        used.append(k)
        return pltpu.make_async_remote_copy(
            src_ref=src, dst_ref=dst, send_sem=zs.at[k], recv_sem=zr.at[k],
            device_id=device, device_id_type=MESH,
        )

    def xy_send(k, src, dst, first=0, width=PW):
        cols = pl.ds(first, width)
        copies = [
            pltpu.make_async_remote_copy(
                src_ref=src.at[pl.ds(16 * q, 16), cols],
                dst_ref=dst.at[pl.ds(16 * inverse(q), 16), cols],
                send_sem=xs.at[k, q],
                recv_sem=xr.at[k, inverse(q)],
                device_id=xy_dev(q),
                device_id_type=MESH,
            )
            for q in NEAR
        ]
        for copy in copies:
            start(copy)
        dst[pl.ds(0, 16), cols] = src[pl.ds(0, 16), cols]
        return copies

    def arrive(copies):
        for copy in copies:
            copy.wait_recv()

    ui = iota((128, 128), 0)
    uj = iota((128, 128), 1)

    def pack_rows(src):
        x3[...] = jnp.zeros((128, PW), BF)
        for j in range(3):
            x3[pl.ds(16 * j, 16), :] = src[:, PW * j : PW * (j + 1)]
        for j in range(5):
            x3[pl.ds(48 + 16 * j, 16), pl.ds(128 * j, 128)] = src[:, 3 * PW : D]

    def pack_notes(notes):
        for j in range(5):
            x3[pl.ds(48 + 16 * j, 16), pl.ds(128 * (5 + j // 2), 128)] = notes[:, pl.ds(128 * (j % 2), 128)]

    def pack_in(mat, dst, first=0, width=PW):
        cols = pl.ds(first, width)
        dst[:, cols] = jnp.dot(mat[...], x3[:, cols], preferred_element_type=F32).astype(BF)

    tiled = jnp.dot(
        routes_t[...].astype(F32).astype(BF),
        one_hot((iota((16, 128), 1) & 15) == iota((16, 128), 0)),
        preferred_element_type=F32,
    )
    amat[...] = route_matrix(tiled.astype(I32), y, x)
    pack_rows(tok)
    pack_in(amat, pack_t, *PIECES[0])

    raw_i = remote(info, info2, z_dev(2))
    raw_t = remote(tok, tok2, z_dev(2))
    raw_u = remote(ups, ups2, z_dev(2))

    pl.semaphore_wait(barrier, 19)
    sent_t = [xy_send(0, pack_t, got_t, *PIECES[0])]

    seq_w = seq_weight(seq_ids, ratios)
    rw = (combine_t[...] * seq_w).astype(BF).astype(F32)
    info[:, pl.ds(256, 128)] = jnp.concatenate([tiled, jnp.zeros((8, 128), F32)], axis=0).astype(BF)
    expert = iota((128, 16), 0)
    same = one_hot(ui == uj)
    for half in range(2):
        acc = jnp.zeros((128, 16), F32)
        for k in range(8):
            acc = acc + jnp.where(routes_t[k : k + 1, :] == expert - 64 * half, rw[k : k + 1, :], 0.0)
        info[:, pl.ds(128 * half, 128)] = lax.dot_general(
            acc.astype(BF), same, TN, preferred_element_type=F32
        ).astype(BF)
    pack_notes(info)
    pack_in(amat, pack_t, *PIECES[1])
    sent_t.append(xy_send(6, pack_t, got_t, *PIECES[1]))
    start(raw_i)
    start(raw_t)
    start(raw_u)
    pack_rows(ups)
    pack_in(amat, pack_u)
    sent_u = xy_send(1, pack_u, got_u)
    for copy in loads:
        copy.start()

    brow = iota((4 * ROWS, 256), 0)
    part = jnp.where(brow >= 80, 1, 0) + jnp.where(brow >= 160, 1, 0) + jnp.where(brow >= 240, 1, 0)
    rem = brow - 80 * part
    bq = (rem * 205) >> 10
    bs = rem - 5 * bq
    bmat[...] = one_hot(iota((4 * ROWS, 256), 1) == bq * 16 + jnp.where(part < 3, 5 * part + bs, 15))
    drow = iota((ROWS, 128), 0)
    dlane = iota((ROWS, 128), 1)
    ds_ = drow - 5 * ((drow * 205) >> 10)
    take = one_hot(((ui & 63) == 3 * node + uj) & (uj < 3))

    def unpack(p, got, dst, place, notes=False):
        first, width = PIECES[p]
        dense = jnp.dot(bmat[...], got[:, pl.ds(first, width)], preferred_element_type=F32)
        for j in range(3):
            dst[place, pl.ds(PW * j + first, width)] = dense[ROWS * j : ROWS * (j + 1), :].astype(BF)
        last = dense[3 * ROWS : 4 * ROWS, :]
        if p == 0:
            tail = jnp.zeros((ROWS, 128), F32)
            for j in range(5):
                tail = jnp.where(ds_ == j, last[:, 128 * j : 128 * (j + 1)], tail)
            dst[place, pl.ds(3 * PW, 128)] = tail.astype(BF)
        elif notes:
            picked = jnp.zeros((ROWS, 128), F32)
            for j in range(5):
                mine = (ds_ == j) & ((dlane >> 6) == j % 2)
                picked = jnp.where(mine, last[:, 128 * (j // 2) : 128 * (1 + j // 2)], picked)
            dst[place, pl.ds(D, 128)] = jnp.dot(picked.astype(BF), take, preferred_element_type=F32).astype(BF)

    def gather_copy(buf, src, dst, device):
        return remote(buf.at[slot(*src), :], buf.at[slot(*dst), :], device)

    def pieces(src, dst, device):
        return [[remote(src(cols), dst(cols), device) for cols in dense_slices(p)] for p in range(2)]

    tp = pieces(lambda cols: xb.at[slot(0, 0), cols], lambda cols: xb.at[slot(3, 0), cols], z_dev(1))
    tm = pieces(lambda cols: xb.at[slot(0, 0), cols], lambda cols: xb.at[slot(1, 0), cols], z_dev(3))
    up = gather_copy(ub, (0, 0), (3, 0), z_dev(1))
    um = gather_copy(ub, (0, 0), (1, 0), z_dev(3))
    t_sib = {dz: gather_copy(xb, (dz, 0), (dz, 1), sib) for dz in range(4)}
    u_sib = {dz: gather_copy(ub, (dz, 0), (dz, 1), sib) for dz in range(4)}

    for p in range(2):
        arrive(sent_t[p])
        unpack(p, got_t, xb, slot(0, 0), True)
        for plus, minus in zip(tp[p], tm[p]):
            start(plus)
            start(minus)
    start(t_sib[0])

    raw_i.wait_recv()
    amat2[...] = route_matrix(info2[:, pl.ds(256, 128)].astype(F32).astype(I32), y, x)
    raw_t.wait_recv()
    pack_rows(tok2)
    pack_notes(info2)
    pack_in(amat2, pack_t2)
    sent_t2 = xy_send(2, pack_t2, got_t2)
    raw_u.wait_recv()
    pack_rows(ups2)
    pack_in(amat2, pack_u2)
    arrive(sent_u)
    sent_u2 = xy_send(3, pack_u2, got_u2)
    for p in range(2):
        unpack(p, got_u, ub, slot(0, 0))
    start(up)
    start(um)
    start(u_sib[0])

    def gate_up(r0, m):
        rows = pl.ds(r0, m)
        for e in range(3):
            pre[rows, pl.ds(256 * e, 256)] = jnp.dot(
                xb[rows, pl.ds(0, D)], wall[:, pl.ds(256 * e, 256)], preferred_element_type=F32
            )

    def backward(r0, m):
        rows = pl.ds(r0, m)
        proj_all = lax.dot_general(ub[rows, :], wdn[...], NT, preferred_element_type=F32)
        score = jnp.zeros((m, 128), F32)
        lanes = iota((m, 128), 1)
        for e in range(3):
            gate = pre[rows, pl.ds(256 * e, 128)]
            upv = pre[rows, pl.ds(256 * e + 128, 128)]
            proj = proj_all[:, 128 * e : 128 * (e + 1)]
            scale = xb[rows, pl.ds(D, 128)][:, e : e + 1].astype(F32)
            sig = jax.nn.sigmoid(gate)
            act = gate * sig
            hidden = (act * upv).astype(BF).astype(F32)
            score = jnp.where(lanes == e, jnp.sum(hidden * proj, axis=1, keepdims=True), score)
            dh = scale * proj
            dall[rows, pl.ds(256 * e, 128)] = (dh * upv * sig * (1.0 + gate * (1.0 - sig))).astype(BF)
            dall[rows, pl.ds(256 * e + 128, 128)] = (dh * act).astype(BF)
            scl[rows, pl.ds(128 * e, 128)] = (hidden * scale).astype(BF)
        pb[rows, pl.ds(D, 128)] = score.astype(BF)

        @pl.loop(0, 7)
        def _(i):
            cols = pl.ds(pl.multiple_of(i * 512, 512), 512)
            pb[rows, cols] = lax.dot_general(
                dall[rows, :], wall[cols, :], NT, preferred_element_type=F32
            ).astype(BF)

    p_sib = {
        dz: remote(pb.at[slot(dz, 1), :], sb.at[pl.ds(POS[dz] * ROWS, ROWS), :], sib)
        for dz in range(4)
    }

    def pair_sum(dz, cols):
        return pb[slot(dz, 0), cols].astype(F32) + sb[pl.ds(POS[dz] * ROWS, ROWS), cols].astype(F32)

    crow = iota((256, 384), 0)
    clane = iota((256, 384), 1)
    cpart = jnp.where(clane >= 80, 1, 0) + jnp.where(clane >= 160, 1, 0) + jnp.where(clane >= 240, 1, 0)
    crem = clane - 80 * cpart
    cq = (crem * 205) >> 10
    cs = crem - 5 * cq
    cmat[...] = one_hot((crow == cq * 16 + jnp.where(cpart < 3, 5 * cpart + cs, 15)) & (clane < 320))
    x4[...] = jnp.zeros((384, PW), BF)
    repeat = one_hot((ui == (uj & 7)) & (ui < 3))

    def pack_out(p, total, dst):
        first, width = PIECES[p]
        slices = dense_slices(p)
        for j in range(3):
            x4[pl.ds(ROWS * j, ROWS), pl.ds(first, width)] = total(slices[j]).astype(BF)
        extra = total(slices[3])
        if p == 0:
            for j in range(5):
                x4[pl.ds(3 * ROWS, ROWS), pl.ds(128 * j, 128)] = jnp.where(ds_ == j, extra, 0.0).astype(BF)
        else:
            score = jnp.dot(extra.astype(BF), repeat, preferred_element_type=F32)
            x4[pl.ds(3 * ROWS, ROWS), pl.ds(640, 128)] = jnp.where((dlane >> 3) == ds_, score, 0.0).astype(BF)
        dst[:, pl.ds(first, width)] = jnp.dot(
            cmat[...], x4[:, pl.ds(first, width)], preferred_element_type=F32
        ).astype(BF)

    for copy in loads:
        copy.wait()
    t_sib[0].wait_recv()
    gate_up(0, 160)
    u_sib[0].wait_recv()
    backward(0, 160)
    start(p_sib[0])

    arrive(tp[0] + tp[1])
    start(t_sib[3])
    arrive(tm[0] + tm[1])
    start(t_sib[1])
    arrive(sent_t2)
    for p in range(2):
        unpack(p, got_t2, xb, slot(2, 0), True)
    start(t_sib[2])
    t_sib[1].wait_recv()
    t_sib[3].wait_recv()
    gate_up(160, 320)
    t_sib[2].wait_recv()
    gate_up(480, 160)
    arrive(sent_u2)
    for p in range(2):
        unpack(p, got_u2, ub, slot(2, 0))
    start(u_sib[2])
    um.wait_recv()
    start(u_sib[1])
    up.wait_recv()
    start(u_sib[3])
    u_sib[2].wait_recv()
    backward(480, 160)
    start(p_sib[2])
    u_sib[1].wait_recv()
    u_sib[3].wait_recv()
    backward(160, 320)
    start(p_sib[1])
    start(p_sib[3])
    r1 = pieces(lambda cols: pb.at[slot(1, 0), cols], lambda cols: fin.at[0, :, cols], z_dev(1))
    r3 = pieces(lambda cols: pb.at[slot(3, 0), cols], lambda cols: fin.at[1, :, cols], z_dev(3))

    def reduce_send(p):
        for dz, copies in ((1, r1), (3, r3)):
            for cols, copy in zip(dense_slices(p), copies[p]):
                pb[slot(dz, 0), cols] = pair_sum(dz, cols).astype(BF)
                start(copy)

    p_sib[1].wait_recv()
    p_sib[3].wait_recv()
    reduce_send(0)
    p_sib[2].wait_recv()
    for p in range(2):
        pack_out(p, lambda cols: pair_sum(2, cols), pack_b2)
    sent_b2 = xy_send(4, pack_b2, got_b2)

    def weight_grads(first, last):
        @pl.loop(first, last)
        def _(i):
            cols = pl.ds(pl.multiple_of(i * 512, 512), 512)
            grads = lax.dot_general(xb[:, cols], dall[...], TN, preferred_element_type=F32).astype(BF)
            for e in range(3):
                gg[e, cols, :] = grads[:, 256 * e : 256 * e + 128]
                gu[e, cols, :] = grads[:, 256 * e + 128 : 256 * (e + 1)]

    def down_grads(first, last):
        @pl.loop(first, last)
        def _(i):
            cols = pl.ds(pl.multiple_of(i * 512, 512), 512)
            grads = lax.dot_general(scl[...], ub[:, cols], TN, preferred_element_type=F32).astype(BF)
            for e in range(3):
                gd[e, :, cols] = grads[128 * e : 128 * (e + 1), :]

    weight_grads(0, 2)
    reduce_send(1)
    weight_grads(2, 5)
    arrive(sent_b2)
    parts, tail, score = token_sums(amat2, got_b2, y, x)
    for j in range(3):
        far_out[:, pl.ds(PW * j, PW)] = parts[j].astype(BF)
    far_out[:, pl.ds(3 * PW, 128)] = tail.astype(BF)
    far_out[:, pl.ds(D, 128)] = score.astype(BF)
    raw_b = remote(far_out, far, z_dev(2))
    start(raw_b)
    p_sib[0].wait_recv()
    sent_b = []
    for p in range(2):
        arrive(r1[p] + r3[p])
        pack_out(
            p, lambda cols: pair_sum(0, cols) + fin[0, :, cols].astype(F32) + fin[1, :, cols].astype(F32), pack_b
        )
        sent_b.append(xy_send(5 + 2 * p, pack_b, got_b, *PIECES[p]))
        if p == 0:
            weight_grads(5, 7)
    down_grads(0, 7)
    raw_b.wait_recv()
    for p in range(2):
        arrive(sent_b[p])
    for copy in started:
        copy.wait_send()


def finish(amat, got_b, far, routes_t, seq_ids, ratios, gg_in, gu_in, gd_in, gt, gc, gg, gu, gd, sems):
    copies = []
    for k, (src, dst) in enumerate(((gg_in, gg), (gu_in, gu), (gd_in, gd))):
        for e in range(3):
            copies.append(pltpu.make_async_copy(src.at[e], dst.at[e], sems.at[3 * k + e]))
    for copy in copies:
        copy.start()
    node = lax.axis_index("node")
    seq_w = seq_weight(seq_ids, ratios)
    parts, tail, score = token_sums(amat, got_b, node // 4, node % 4)
    for j in range(3):
        gt[:, pl.ds(PW * j, PW)] = (parts[j] + far[:, pl.ds(PW * j, PW)].astype(F32)).astype(BF)
    gt[:, pl.ds(3 * PW, 128)] = (tail + far[:, pl.ds(3 * PW, 128)].astype(F32)).astype(BF)
    score = score + far[:, pl.ds(D, 128)].astype(F32)
    eye = one_hot(iota((16, 16), 0) == iota((16, 16), 1))
    scores = lax.dot_general(score.astype(BF), eye, TN, preferred_element_type=F32)
    expert = iota((128, 16), 0)
    for k in range(8):
        value = jnp.sum(jnp.where(routes_t[k : k + 1, :] == expert, scores, 0.0), axis=0, keepdims=True)
        gc[pl.ds(k, 1), :] = value * seq_w[k : k + 1, :]
    for copy in copies:
        copy.wait()


def local(tokens, upstream, routes, combine, seq_ids, ratios, w_gate, w_up, w_down):
    vmem = pl.BlockSpec(memory_space=pltpu.VMEM)
    hbm = pl.BlockSpec(memory_space=pl.ANY)
    shape = jax.ShapeDtypeStruct
    dma = pltpu.SemaphoreType.DMA
    routes_t, combine_t, seq_ids, ratios = routes.T, combine.T, seq_ids[None, :], ratios[None, :]
    amat, got_b, far, *grads = pl.pallas_call(
        kernel,
        out_shape=(
            pltpu.VMEM((256, 128), BF),
            pltpu.VMEM((256, PW), BF),
            pltpu.VMEM((16, DT), BF),
            pltpu.VMEM((3, D, 128), BF),
            pltpu.VMEM((3, D, 128), BF),
            pltpu.VMEM((3, 128, D), BF),
        ),
        in_specs=[vmem] * 6 + [hbm] * 3,
        out_specs=(vmem,) * 6,
        scratch_shapes=[
            pltpu.VMEM((256, 128), BF),
            pltpu.VMEM((320, 256), BF),
            pltpu.VMEM((256, 384), BF),
            pltpu.VMEM((128, PW), BF),
            pltpu.VMEM((16, 384), BF),
            pltpu.VMEM((16, D), BF),
            pltpu.VMEM((16, D), BF),
            pltpu.VMEM((16, 384), BF),
            pltpu.VMEM((16, DT), BF),
        ]
        + [pltpu.VMEM((256, PW), BF)] * 11
        + [
            pltpu.VMEM((640, DT), BF),
            pltpu.VMEM((640, D), BF),
            pltpu.VMEM((D, 768), BF),
            pltpu.VMEM((384, D), BF),
            pltpu.VMEM((640, 768), F32),
            pltpu.VMEM((640, 768), BF),
            pltpu.VMEM((640, 384), BF),
            pltpu.VMEM((640, DT), BF),
            pltpu.VMEM((320, DT), BF),
            pltpu.VMEM((2, ROWS, DT), BF),
            pltpu.VMEM((384, PW), BF),
            dma((9,)), dma((8, 16)), dma((8, 16)), dma((64,)), dma((64,)),
        ],
        compiler_params=pltpu.CompilerParams(
            collective_id=0, has_side_effects=True, vmem_limit_bytes=46 << 20
        ),
        name="moe_grad",
    )(tokens, upstream, routes_t, combine_t, seq_ids, ratios, w_gate, w_up, w_down)
    gt, gc, gg, gu, gd = pl.pallas_call(
        finish,
        out_shape=(
            shape((16, D), BF),
            shape((8, 16), F32),
            shape((3, D, 128), BF),
            shape((3, D, 128), BF),
            shape((3, 128, D), BF),
        ),
        in_specs=[vmem] * 9,
        out_specs=(vmem, vmem, hbm, hbm, hbm),
        scratch_shapes=[dma((9,))],
        compiler_params=pltpu.CompilerParams(vmem_limit_bytes=16 << 20),
        name="moe_finish",
    )(amat, got_b, far, routes_t, seq_ids, ratios, *grads)
    return gt, gc.T, gg, gu, gd


def solution(mesh):
    rows = P(("node", "local"), None)
    return jax.shard_map(
        local,
        mesh=mesh,
        in_specs=(
            rows, rows, rows, rows, P(("node", "local")), P(),
            P("node", None, "local"), P("node", None, "local"), P("node", "local", None),
        ),
        out_specs=(rows, rows, P("node", None, "local"), P("node", None, "local"), P("node", "local", None)),
        check_vma=False,
    )
```

```python
import jax
import jax.numpy as jnp
from jax import lax
from jax.experimental import pallas as pl
from jax.experimental.pallas import tpu as pltpu
from jax.sharding import PartitionSpec as P

MESH = pl.DeviceIdType.MESH
BF = jnp.bfloat16
F32 = jnp.float32
I32 = jnp.int32

D = 3584
DT = D + 128
CA = 1792
PW = 1152
ROWS = 80
POS = {0: 0, 1: 1, 3: 2, 2: 3}
NEAR = (1, 3, 4, 12, 2, 5, 7, 8, 13, 15, 6, 9, 11, 14, 10)
PIECES = ((0, 640), (640, 512))
NT = (((1,), (1,)), ((), ()))
TN = (((0,), (0,)), ((), ()))


def slot(dz, dc):
    return pl.ds((POS[dz] * 2 + dc) * ROWS, ROWS)


def dense_slices(p):
    first, width = PIECES[p]
    return [pl.ds(PW * j + first, width) for j in range(3)] + [pl.ds(3 * PW + 128 * p, 128)]


def inverse(q):
    return ((-(q // 4)) % 4) * 4 + (-(q % 4)) % 4


def iota(shape, dim):
    return lax.broadcasted_iota(I32, shape, dim)


def one_hot(mask):
    return jnp.where(mask, 1.0, 0.0).astype(BF)


def seq_weight(seq_ids, ratios):
    hot = jnp.where(iota((256, 16), 0) == seq_ids[...], 1.0, 0.0)
    clipped = jnp.broadcast_to(jnp.minimum(ratios[...], 1.0), (8, 256))
    return jnp.dot(clipped, hot, precision=lax.Precision.HIGHEST, preferred_element_type=F32)


def route_matrix(tiled, y, x):
    row = iota((256, 128), 0)
    lane = iota((256, 128), 1)
    r = row & 15
    blk = lane >> 4
    lo = first_expert(row, y, x)
    hit = jnp.zeros((256, 128), F32)
    for k in range(8):
        rk = tiled[k : k + 1, :]
        hit = jnp.where((rk >= lo) & (rk < lo + 3), 1.0, hit)
    ui = iota((128, 128), 0)
    uj = iota((128, 128), 1)
    before = one_hot(((ui >> 4) == (uj >> 4)) & ((ui & 15) < (uj & 15)))
    place = jnp.dot(hit.astype(BF), before, preferred_element_type=F32).astype(I32)
    want = jnp.where(blk < 3, jnp.where(r < 15, r - 5 * blk, -1), jnp.where(r == 15, blk - 3, -1))
    return one_hot((hit > 0.5) & (place == want) & (want >= 0) & (want < 5))


def first_expert(row, y, x):
    q = row >> 4
    return 3 * ((((y + (q >> 2)) & 3) << 2) + ((x + (q & 3)) & 3))


def token_sums(amat, got, y, x):
    row = iota((256, 128), 0)
    lane = iota((256, 128), 1)
    lo = first_expert(row, y, x)
    summed = lax.dot_general(amat[...], got[...], TN, preferred_element_type=F32)
    parts = [summed[16 * j : 16 * (j + 1), :] for j in range(3)]
    tail = jnp.zeros((16, 128), F32)
    for j in range(5):
        tail = tail + summed[48 + 16 * j : 64 + 16 * j, 128 * j : 128 * (j + 1)]
    ui = iota((128, 128), 0)
    uj = iota((128, 128), 1)
    third = uj - 3 * ((uj * 171) >> 9)
    score = jnp.zeros((16, 128), F32)
    for j in range(5):
        pick = one_hot(ui == 8 * j + third)
        wide = jnp.dot(got[:, pl.ds(640, 128)], pick, preferred_element_type=F32)
        wide = jnp.where((lane >= lo) & (lane < lo + 3), wide, 0.0).astype(BF)
        share = lax.dot_general(amat[...], wide, TN, preferred_element_type=F32)
        score = score + share[48 + 16 * j : 64 + 16 * j, :]
    return parts, tail, score


def kernel(
    tok, ups, routes_t, combine_t, seq_ids, ratios, wg, wu, wd,
    amat, got_b, far, gg, gu, gd,
    amat2, bmat, cmat, x3, info, tok2, ups2, info2, far_out,
    pack_t, pack_u, pack_t2, pack_u2, pack_b, pack_b2, got_t, got_u, got_t2, got_u2, got_b2,
    xb, ub, wall, wdn, pre, dall, scl, pb, sb, fin, x4,
    wsem, xs, xr, zs, zr,
):
    node = lax.axis_index("node")
    loc = lax.axis_index("local")
    y, x = node // 4, node % 4
    z, c = loc // 2, loc % 2

    def xy_dev(q):
        return (((y + q // 4) % 4) * 4 + (x + q % 4) % 4, loc)

    def z_dev(dz):
        return (node, ((z + dz) % 4) * 2 + c)

    sib = (node, z * 2 + 1 - c)

    loads = []
    for e in range(3):
        loads.append(pltpu.make_async_copy(wg.at[e], wall.at[:, pl.ds(256 * e, 128)], wsem.at[3 * e]))
        loads.append(pltpu.make_async_copy(wu.at[e], wall.at[:, pl.ds(256 * e + 128, 128)], wsem.at[3 * e + 1]))
        loads.append(pltpu.make_async_copy(wd.at[e], wdn.at[pl.ds(128 * e, 128), :], wsem.at[3 * e + 2]))

    barrier = pltpu.get_barrier_semaphore()
    for q in range(1, 16):
        pl.semaphore_signal(barrier, inc=1, device_id=xy_dev(q), device_id_type=MESH)
    for peer in (z_dev(1), z_dev(2), z_dev(3), sib):
        pl.semaphore_signal(barrier, inc=1, device_id=peer, device_id_type=MESH)

    started = []

    def start(copy):
        copy.start()
        started.append(copy)

    used = []

    def remote(src, dst, device):
        k = len(used)
        used.append(k)
        return pltpu.make_async_remote_copy(
            src_ref=src, dst_ref=dst, send_sem=zs.at[k], recv_sem=zr.at[k],
            device_id=device, device_id_type=MESH,
        )

    def xy_send(k, src, dst, first=0, width=PW):
        cols = pl.ds(first, width)
        copies = [
            pltpu.make_async_remote_copy(
                src_ref=src.at[pl.ds(16 * q, 16), cols],
                dst_ref=dst.at[pl.ds(16 * inverse(q), 16), cols],
                send_sem=xs.at[k, q],
                recv_sem=xr.at[k, inverse(q)],
                device_id=xy_dev(q),
                device_id_type=MESH,
            )
            for q in NEAR
        ]
        for copy in copies:
            start(copy)
        dst[pl.ds(0, 16), cols] = src[pl.ds(0, 16), cols]
        return copies

    def arrive(copies):
        for copy in copies:
            copy.wait_recv()

    ui = iota((128, 128), 0)
    uj = iota((128, 128), 1)

    def pack_rows(src):
        x3[...] = jnp.zeros((128, PW), BF)
        for j in range(3):
            x3[pl.ds(16 * j, 16), :] = src[:, PW * j : PW * (j + 1)]
        for j in range(5):
            x3[pl.ds(48 + 16 * j, 16), pl.ds(128 * j, 128)] = src[:, 3 * PW : D]

    def pack_notes(notes):
        for j in range(5):
            x3[pl.ds(48 + 16 * j, 16), pl.ds(128 * (5 + j // 2), 128)] = notes[:, pl.ds(128 * (j % 2), 128)]

    def pack_in(mat, dst, first=0, width=PW):
        cols = pl.ds(first, width)
        dst[:, cols] = jnp.dot(mat[...], x3[:, cols], preferred_element_type=F32).astype(BF)

    tiled = jnp.dot(
        routes_t[...].astype(F32).astype(BF),
        one_hot((iota((16, 128), 1) & 15) == iota((16, 128), 0)),
        preferred_element_type=F32,
    )
    amat[...] = route_matrix(tiled.astype(I32), y, x)
    pack_rows(tok)
    pack_in(amat, pack_t, *PIECES[0])

    raw_i = remote(info, info2, z_dev(2))
    raw_t = remote(tok, tok2, z_dev(2))
    raw_u = remote(ups, ups2, z_dev(2))

    pl.semaphore_wait(barrier, 19)
    sent_t = [xy_send(0, pack_t, got_t, *PIECES[0])]

    seq_w = seq_weight(seq_ids, ratios)
    rw = (combine_t[...] * seq_w).astype(BF).astype(F32)
    info[:, pl.ds(256, 128)] = jnp.concatenate([tiled, jnp.zeros((8, 128), F32)], axis=0).astype(BF)
    expert = iota((128, 16), 0)
    same = one_hot(ui == uj)
    for half in range(2):
        acc = jnp.zeros((128, 16), F32)
        for k in range(8):
            acc = acc + jnp.where(routes_t[k : k + 1, :] == expert - 64 * half, rw[k : k + 1, :], 0.0)
        info[:, pl.ds(128 * half, 128)] = lax.dot_general(
            acc.astype(BF), same, TN, preferred_element_type=F32
        ).astype(BF)
    pack_notes(info)
    pack_in(amat, pack_t, *PIECES[1])
    sent_t.append(xy_send(6, pack_t, got_t, *PIECES[1]))
    start(raw_i)
    start(raw_t)
    start(raw_u)
    pack_rows(ups)
    pack_in(amat, pack_u)
    sent_u = xy_send(1, pack_u, got_u)
    for copy in loads:
        copy.start()

    brow = iota((4 * ROWS, 256), 0)
    part = jnp.where(brow >= 80, 1, 0) + jnp.where(brow >= 160, 1, 0) + jnp.where(brow >= 240, 1, 0)
    rem = brow - 80 * part
    bq = (rem * 205) >> 10
    bs = rem - 5 * bq
    bmat[...] = one_hot(iota((4 * ROWS, 256), 1) == bq * 16 + jnp.where(part < 3, 5 * part + bs, 15))
    drow = iota((ROWS, 128), 0)
    dlane = iota((ROWS, 128), 1)
    ds_ = drow - 5 * ((drow * 205) >> 10)
    take = one_hot(((ui & 63) == 3 * node + uj) & (uj < 3))

    def unpack(p, got, dst, place, notes=False):
        first, width = PIECES[p]
        dense = jnp.dot(bmat[...], got[:, pl.ds(first, width)], preferred_element_type=F32)
        for j in range(3):
            dst[place, pl.ds(PW * j + first, width)] = dense[ROWS * j : ROWS * (j + 1), :].astype(BF)
        last = dense[3 * ROWS : 4 * ROWS, :]
        if p == 0:
            tail = jnp.zeros((ROWS, 128), F32)
            for j in range(5):
                tail = jnp.where(ds_ == j, last[:, 128 * j : 128 * (j + 1)], tail)
            dst[place, pl.ds(3 * PW, 128)] = tail.astype(BF)
        elif notes:
            picked = jnp.zeros((ROWS, 128), F32)
            for j in range(5):
                mine = (ds_ == j) & ((dlane >> 6) == j % 2)
                picked = jnp.where(mine, last[:, 128 * (j // 2) : 128 * (1 + j // 2)], picked)
            dst[place, pl.ds(D, 128)] = jnp.dot(picked.astype(BF), take, preferred_element_type=F32).astype(BF)

    def gather_copy(buf, src, dst, device):
        return remote(buf.at[slot(*src), :], buf.at[slot(*dst), :], device)

    def pieces(src, dst, device):
        return [[remote(src(cols), dst(cols), device) for cols in dense_slices(p)] for p in range(2)]

    tp = pieces(lambda cols: xb.at[slot(0, 0), cols], lambda cols: xb.at[slot(3, 0), cols], z_dev(1))
    tm = pieces(lambda cols: xb.at[slot(0, 0), cols], lambda cols: xb.at[slot(1, 0), cols], z_dev(3))
    def half_copies(src, dst, device):
        return [remote(src(cols), dst(cols), device) for cols in (pl.ds(0, CA), pl.ds(CA, D - CA))]

    up = half_copies(lambda cols: ub.at[slot(0, 0), cols], lambda cols: ub.at[slot(3, 0), cols], z_dev(1))
    um = half_copies(lambda cols: ub.at[slot(0, 0), cols], lambda cols: ub.at[slot(1, 0), cols], z_dev(3))
    t_sib = {dz: gather_copy(xb, (dz, 0), (dz, 1), sib) for dz in range(4)}
    u_sib = {dz: gather_copy(ub, (dz, 0), (dz, 1), sib) for dz in (0, 2)}
    for dz in (1, 3):
        u_sib[dz] = half_copies(
            lambda cols, dz=dz: ub.at[slot(dz, 0), cols], lambda cols, dz=dz: ub.at[slot(dz, 1), cols], sib
        )

    for p in range(2):
        arrive(sent_t[p])
        unpack(p, got_t, xb, slot(0, 0), True)
        for plus, minus in zip(tp[p], tm[p]):
            start(plus)
            start(minus)
    start(t_sib[0])

    raw_i.wait_recv()
    amat2[...] = route_matrix(info2[:, pl.ds(256, 128)].astype(F32).astype(I32), y, x)
    raw_t.wait_recv()
    pack_rows(tok2)
    pack_notes(info2)
    pack_in(amat2, pack_t2)
    sent_t2 = xy_send(2, pack_t2, got_t2)
    raw_u.wait_recv()
    pack_rows(ups2)
    pack_in(amat2, pack_u2)
    arrive(sent_u)
    sent_u2 = xy_send(3, pack_u2, got_u2)
    for p in range(2):
        unpack(p, got_u, ub, slot(0, 0))
    for h in range(2):
        start(up[h])
        start(um[h])
    start(u_sib[0])

    def gate_up(r0, m):
        rows = pl.ds(r0, m)
        for e in range(3):
            pre[rows, pl.ds(256 * e, 256)] = jnp.dot(
                xb[rows, pl.ds(0, D)], wall[:, pl.ds(256 * e, 256)], preferred_element_type=F32
            )

    def backward(r0, m, chips):
        rows = pl.ds(r0, m)
        proj_all = lax.dot_general(ub[rows, :], wdn[...], NT, preferred_element_type=F32)
        score = jnp.zeros((m, 128), F32)
        lanes = iota((m, 128), 1)
        for e in range(3):
            gate = pre[rows, pl.ds(256 * e, 128)]
            upv = pre[rows, pl.ds(256 * e + 128, 128)]
            proj = proj_all[:, 128 * e : 128 * (e + 1)]
            scale = xb[rows, pl.ds(D, 128)][:, e : e + 1].astype(F32)
            sig = jax.nn.sigmoid(gate)
            act = gate * sig
            hidden = (act * upv).astype(BF).astype(F32)
            score = jnp.where(lanes == e, jnp.sum(hidden * proj, axis=1, keepdims=True), score)
            dh = scale * proj
            dall[rows, pl.ds(256 * e, 128)] = (dh * upv * sig * (1.0 + gate * (1.0 - sig))).astype(BF)
            dall[rows, pl.ds(256 * e + 128, 128)] = (dh * act).astype(BF)
            scl[rows, pl.ds(128 * e, 128)] = (hidden * scale).astype(BF)
        pb[rows, pl.ds(D, 128)] = score.astype(BF)

        def partial(first, last):
            @pl.loop(first, last)
            def _(i):
                cols = pl.ds(pl.multiple_of(i * 512, 512), 512)
                pb[rows, cols] = lax.dot_general(
                    dall[rows, :], wall[cols, :], NT, preferred_element_type=F32
                ).astype(BF)

        partial(0, 4)
        for dz in chips:
            start(p_sib[dz][0])
        partial(4, 7)
        for dz in chips:
            start(p_sib[dz][1])

    p_sib = {
        dz: [
            remote(pb.at[slot(dz, 1), cols], sb.at[pl.ds(POS[dz] * ROWS, ROWS), cols], sib)
            for cols in (pl.ds(0, 2048), pl.ds(2048, DT - 2048))
        ]
        for dz in range(4)
    }

    def pair_sum(dz, cols):
        return pb[slot(dz, 0), cols].astype(F32) + sb[pl.ds(POS[dz] * ROWS, ROWS), cols].astype(F32)

    crow = iota((256, 384), 0)
    clane = iota((256, 384), 1)
    cpart = jnp.where(clane >= 80, 1, 0) + jnp.where(clane >= 160, 1, 0) + jnp.where(clane >= 240, 1, 0)
    crem = clane - 80 * cpart
    cq = (crem * 205) >> 10
    cs = crem - 5 * cq
    cmat[...] = one_hot((crow == cq * 16 + jnp.where(cpart < 3, 5 * cpart + cs, 15)) & (clane < 320))
    x4[...] = jnp.zeros((384, PW), BF)
    repeat = one_hot((ui == (uj & 7)) & (ui < 3))

    def pack_out(p, total, dst):
        first, width = PIECES[p]
        slices = dense_slices(p)
        for j in range(3):
            x4[pl.ds(ROWS * j, ROWS), pl.ds(first, width)] = total(slices[j]).astype(BF)
        extra = total(slices[3])
        if p == 0:
            for j in range(5):
                x4[pl.ds(3 * ROWS, ROWS), pl.ds(128 * j, 128)] = jnp.where(ds_ == j, extra, 0.0).astype(BF)
        else:
            score = jnp.dot(extra.astype(BF), repeat, preferred_element_type=F32)
            x4[pl.ds(3 * ROWS, ROWS), pl.ds(640, 128)] = jnp.where((dlane >> 3) == ds_, score, 0.0).astype(BF)
        dst[:, pl.ds(first, width)] = jnp.dot(
            cmat[...], x4[:, pl.ds(first, width)], preferred_element_type=F32
        ).astype(BF)

    for copy in loads:
        copy.wait()
    t_sib[0].wait_recv()
    gate_up(0, 160)

    arrive(tp[0] + tp[1])
    start(t_sib[3])
    arrive(tm[0] + tm[1])
    start(t_sib[1])
    arrive(sent_t2)
    for p in range(2):
        unpack(p, got_t2, xb, slot(2, 0), True)
    start(t_sib[2])
    t_sib[1].wait_recv()
    t_sib[3].wait_recv()
    gate_up(160, 320)
    t_sib[2].wait_recv()
    gate_up(480, 160)
    arrive(sent_u2)
    for p in range(2):
        unpack(p, got_u2, ub, slot(2, 0))
    start(u_sib[2])
    for h in range(2):
        um[h].wait_recv()
        start(u_sib[1][h])
        up[h].wait_recv()
        start(u_sib[3][h])
    u_sib[2].wait_recv()
    backward(480, 160, (2,))
    arrive(u_sib[1] + u_sib[3])
    backward(160, 320, (1, 3))
    r1 = pieces(lambda cols: pb.at[slot(1, 0), cols], lambda cols: fin.at[0, :, cols], z_dev(1))
    r3 = pieces(lambda cols: pb.at[slot(3, 0), cols], lambda cols: fin.at[1, :, cols], z_dev(3))

    def reduce_send(p):
        for dz, copies in ((1, r1), (3, r3)):
            for cols, copy in zip(dense_slices(p), copies[p]):
                pb[slot(dz, 0), cols] = pair_sum(dz, cols).astype(BF)
                start(copy)

    arrive(p_sib[1] + p_sib[3])
    reduce_send(0)
    arrive(p_sib[2])
    for p in range(2):
        pack_out(p, lambda cols: pair_sum(2, cols), pack_b2)
    sent_b2 = xy_send(4, pack_b2, got_b2)

    def weight_grads(first, last):
        @pl.loop(first, last)
        def _(i):
            cols = pl.ds(pl.multiple_of(i * 512, 512), 512)
            grads = lax.dot_general(xb[:, cols], dall[...], TN, preferred_element_type=F32).astype(BF)
            for e in range(3):
                gg[e, cols, :] = grads[:, 256 * e : 256 * e + 128]
                gu[e, cols, :] = grads[:, 256 * e + 128 : 256 * (e + 1)]

    def down_grads(first, last):
        @pl.loop(first, last)
        def _(i):
            cols = pl.ds(pl.multiple_of(i * 512, 512), 512)
            grads = lax.dot_general(scl[...], ub[:, cols], TN, preferred_element_type=F32).astype(BF)
            for e in range(3):
                gd[e, :, cols] = grads[128 * e : 128 * (e + 1), :]

    u_sib[0].wait_recv()
    backward(0, 160, (0,))
    weight_grads(0, 1)
    reduce_send(1)
    weight_grads(1, 2)
    weight_grads(2, 5)
    arrive(sent_b2)
    parts, tail, score = token_sums(amat2, got_b2, y, x)
    for j in range(3):
        far_out[:, pl.ds(PW * j, PW)] = parts[j].astype(BF)
    far_out[:, pl.ds(3 * PW, 128)] = tail.astype(BF)
    far_out[:, pl.ds(D, 128)] = score.astype(BF)
    raw_b = remote(far_out, far, z_dev(2))
    start(raw_b)
    arrive(p_sib[0])
    sent_b = []
    for p in range(2):
        arrive(r1[p] + r3[p])
        pack_out(
            p, lambda cols: pair_sum(0, cols) + fin[0, :, cols].astype(F32) + fin[1, :, cols].astype(F32), pack_b
        )
        sent_b.append(xy_send(5 + 2 * p, pack_b, got_b, *PIECES[p]))
        if p == 0:
            weight_grads(5, 7)
    down_grads(0, 7)
    raw_b.wait_recv()
    for p in range(2):
        arrive(sent_b[p])
    for copy in started:
        copy.wait_send()


def finish(amat, got_b, far, routes_t, seq_ids, ratios, gg_in, gu_in, gd_in, gt, gc, gg, gu, gd, sems):
    copies = []
    for k, (src, dst) in enumerate(((gg_in, gg), (gu_in, gu), (gd_in, gd))):
        for e in range(3):
            copies.append(pltpu.make_async_copy(src.at[e], dst.at[e], sems.at[3 * k + e]))
    for copy in copies:
        copy.start()
    node = lax.axis_index("node")
    seq_w = seq_weight(seq_ids, ratios)
    parts, tail, score = token_sums(amat, got_b, node // 4, node % 4)
    for j in range(3):
        gt[:, pl.ds(PW * j, PW)] = (parts[j] + far[:, pl.ds(PW * j, PW)].astype(F32)).astype(BF)
    gt[:, pl.ds(3 * PW, 128)] = (tail + far[:, pl.ds(3 * PW, 128)].astype(F32)).astype(BF)
    score = score + far[:, pl.ds(D, 128)].astype(F32)
    eye = one_hot(iota((16, 16), 0) == iota((16, 16), 1))
    scores = lax.dot_general(score.astype(BF), eye, TN, preferred_element_type=F32)
    expert = iota((128, 16), 0)
    for k in range(8):
        value = jnp.sum(jnp.where(routes_t[k : k + 1, :] == expert, scores, 0.0), axis=0, keepdims=True)
        gc[pl.ds(k, 1), :] = value * seq_w[k : k + 1, :]
    for copy in copies:
        copy.wait()


def local(tokens, upstream, routes, combine, seq_ids, ratios, w_gate, w_up, w_down):
    vmem = pl.BlockSpec(memory_space=pltpu.VMEM)
    hbm = pl.BlockSpec(memory_space=pl.ANY)
    shape = jax.ShapeDtypeStruct
    dma = pltpu.SemaphoreType.DMA
    routes_t, combine_t, seq_ids, ratios = routes.T, combine.T, seq_ids[None, :], ratios[None, :]
    amat, got_b, far, *grads = pl.pallas_call(
        kernel,
        out_shape=(
            pltpu.VMEM((256, 128), BF),
            pltpu.VMEM((256, PW), BF),
            pltpu.VMEM((16, DT), BF),
            pltpu.VMEM((3, D, 128), BF),
            pltpu.VMEM((3, D, 128), BF),
            pltpu.VMEM((3, 128, D), BF),
        ),
        in_specs=[vmem] * 6 + [hbm] * 3,
        out_specs=(vmem,) * 6,
        scratch_shapes=[
            pltpu.VMEM((256, 128), BF),
            pltpu.VMEM((320, 256), BF),
            pltpu.VMEM((256, 384), BF),
            pltpu.VMEM((128, PW), BF),
            pltpu.VMEM((16, 384), BF),
            pltpu.VMEM((16, D), BF),
            pltpu.VMEM((16, D), BF),
            pltpu.VMEM((16, 384), BF),
            pltpu.VMEM((16, DT), BF),
        ]
        + [pltpu.VMEM((256, PW), BF)] * 11
        + [
            pltpu.VMEM((640, DT), BF),
            pltpu.VMEM((640, D), BF),
            pltpu.VMEM((D, 768), BF),
            pltpu.VMEM((384, D), BF),
            pltpu.VMEM((640, 768), F32),
            pltpu.VMEM((640, 768), BF),
            pltpu.VMEM((640, 384), BF),
            pltpu.VMEM((640, DT), BF),
            pltpu.VMEM((320, DT), BF),
            pltpu.VMEM((2, ROWS, DT), BF),
            pltpu.VMEM((384, PW), BF),
            dma((9,)), dma((8, 16)), dma((8, 16)), dma((64,)), dma((64,)),
        ],
        compiler_params=pltpu.CompilerParams(
            collective_id=0, has_side_effects=True, vmem_limit_bytes=46 << 20
        ),
        name="moe_grad",
    )(tokens, upstream, routes_t, combine_t, seq_ids, ratios, w_gate, w_up, w_down)
    gt, gc, gg, gu, gd = pl.pallas_call(
        finish,
        out_shape=(
            shape((16, D), BF),
            shape((8, 16), F32),
            shape((3, D, 128), BF),
            shape((3, D, 128), BF),
            shape((3, 128, D), BF),
        ),
        in_specs=[vmem] * 9,
        out_specs=(vmem, vmem, hbm, hbm, hbm),
        scratch_shapes=[dma((9,))],
        compiler_params=pltpu.CompilerParams(vmem_limit_bytes=16 << 20),
        name="moe_finish",
    )(amat, got_b, far, routes_t, seq_ids, ratios, *grads)
    return gt, gc.T, gg, gu, gd


def solution(mesh):
    rows = P(("node", "local"), None)
    return jax.shard_map(
        local,
        mesh=mesh,
        in_specs=(
            rows, rows, rows, rows, P(("node", "local")), P(),
            P("node", None, "local"), P("node", None, "local"), P("node", "local", None),
        ),
        out_specs=(rows, rows, P("node", None, "local"), P("node", None, "local"), P("node", "local", None)),
        check_vma=False,
    )
```

```python
import jax
import jax.numpy as jnp
from jax import lax
from jax.experimental import pallas as pl
from jax.experimental.pallas import tpu as pltpu
from jax.sharding import PartitionSpec as P

MESH = pl.DeviceIdType.MESH
BF = jnp.bfloat16
F32 = jnp.float32
I32 = jnp.int32

D = 3584
DT = D + 128
CA = 1792
PW = 1152
ROWS = 80
POS = {0: 0, 1: 1, 3: 2, 2: 3}
NEAR = (1, 3, 4, 12, 2, 5, 7, 8, 13, 15, 6, 9, 11, 14, 10)
PIECES = ((0, 640), (640, 512))
NT = (((1,), (1,)), ((), ()))
TN = (((0,), (0,)), ((), ()))


def slot(dz, dc):
    return pl.ds((POS[dz] * 2 + dc) * ROWS, ROWS)


def dense_slices(p):
    first, width = PIECES[p]
    return [pl.ds(PW * j + first, width) for j in range(3)] + [pl.ds(3 * PW + 128 * p, 128)]


def inverse(q):
    return ((-(q // 4)) % 4) * 4 + (-(q % 4)) % 4


def iota(shape, dim):
    return lax.broadcasted_iota(I32, shape, dim)


def one_hot(mask):
    return jnp.where(mask, 1.0, 0.0).astype(BF)


def seq_weight(seq_ids, ratios):
    hot = jnp.where(iota((256, 16), 0) == seq_ids[...], 1.0, 0.0)
    clipped = jnp.broadcast_to(jnp.minimum(ratios[...], 1.0), (8, 256))
    return jnp.dot(clipped, hot, precision=lax.Precision.HIGHEST, preferred_element_type=F32)


def route_matrix(tiled, y, x):
    row = iota((256, 128), 0)
    lane = iota((256, 128), 1)
    r = row & 15
    blk = lane >> 4
    lo = first_expert(row, y, x)
    hit = jnp.zeros((256, 128), F32)
    for k in range(8):
        rk = tiled[k : k + 1, :]
        hit = jnp.where((rk >= lo) & (rk < lo + 3), 1.0, hit)
    ui = iota((128, 128), 0)
    uj = iota((128, 128), 1)
    before = one_hot(((ui >> 4) == (uj >> 4)) & ((ui & 15) < (uj & 15)))
    place = jnp.dot(hit.astype(BF), before, preferred_element_type=F32).astype(I32)
    want = jnp.where(blk < 3, jnp.where(r < 15, r - 5 * blk, -1), jnp.where(r == 15, blk - 3, -1))
    return one_hot((hit > 0.5) & (place == want) & (want >= 0) & (want < 5))


def first_expert(row, y, x):
    q = row >> 4
    return 3 * ((((y + (q >> 2)) & 3) << 2) + ((x + (q & 3)) & 3))


def token_sums(amat, got, y, x):
    row = iota((256, 128), 0)
    lane = iota((256, 128), 1)
    lo = first_expert(row, y, x)
    summed = lax.dot_general(amat[...], got[...], TN, preferred_element_type=F32)
    parts = [summed[16 * j : 16 * (j + 1), :] for j in range(3)]
    tail = jnp.zeros((16, 128), F32)
    for j in range(5):
        tail = tail + summed[48 + 16 * j : 64 + 16 * j, 128 * j : 128 * (j + 1)]
    ui = iota((128, 128), 0)
    uj = iota((128, 128), 1)
    third = uj - 3 * ((uj * 171) >> 9)
    score = jnp.zeros((16, 128), F32)
    for j in range(5):
        pick = one_hot(ui == 8 * j + third)
        wide = jnp.dot(got[:, pl.ds(640, 128)], pick, preferred_element_type=F32)
        wide = jnp.where((lane >= lo) & (lane < lo + 3), wide, 0.0).astype(BF)
        share = lax.dot_general(amat[...], wide, TN, preferred_element_type=F32)
        score = score + share[48 + 16 * j : 64 + 16 * j, :]
    return parts, tail, score


def kernel(
    tok, ups, routes_t, combine_t, seq_ids, ratios, wg, wu, wd,
    amat, got_b, far, gg, gu, gd,
    amat2, bmat, cmat, x3, info, tok2, ups2, info2, far_out,
    pack_t, pack_u, pack_t2, pack_u2, pack_b, pack_b2, got_t, got_u, got_t2, got_u2, got_b2,
    xb, ub, wall, wdn, pre, dall, scl, pb, sb, fin, x4,
    wsem, xs, xr, zs, zr,
):
    node = lax.axis_index("node")
    loc = lax.axis_index("local")
    y, x = node // 4, node % 4
    z, c = loc // 2, loc % 2

    def xy_dev(q):
        return (((y + q // 4) % 4) * 4 + (x + q % 4) % 4, loc)

    def z_dev(dz):
        return (node, ((z + dz) % 4) * 2 + c)

    sib = (node, z * 2 + 1 - c)

    loads = []
    for e in range(3):
        loads.append(pltpu.make_async_copy(wg.at[e], wall.at[:, pl.ds(256 * e, 128)], wsem.at[3 * e]))
        loads.append(pltpu.make_async_copy(wu.at[e], wall.at[:, pl.ds(256 * e + 128, 128)], wsem.at[3 * e + 1]))
        loads.append(pltpu.make_async_copy(wd.at[e], wdn.at[pl.ds(128 * e, 128), :], wsem.at[3 * e + 2]))

    barrier = pltpu.get_barrier_semaphore()
    for q in range(1, 16):
        pl.semaphore_signal(barrier, inc=1, device_id=xy_dev(q), device_id_type=MESH)
    for peer in (z_dev(1), z_dev(2), z_dev(3), sib):
        pl.semaphore_signal(barrier, inc=1, device_id=peer, device_id_type=MESH)

    started = []

    def start(copy):
        copy.start()
        started.append(copy)

    used = []

    def remote(src, dst, device):
        k = len(used)
        used.append(k)
        return pltpu.make_async_remote_copy(
            src_ref=src, dst_ref=dst, send_sem=zs.at[k], recv_sem=zr.at[k],
            device_id=device, device_id_type=MESH,
        )

    def xy_send(k, src, dst, first=0, width=PW):
        cols = pl.ds(first, width)
        copies = [
            pltpu.make_async_remote_copy(
                src_ref=src.at[pl.ds(16 * q, 16), cols],
                dst_ref=dst.at[pl.ds(16 * inverse(q), 16), cols],
                send_sem=xs.at[k, q],
                recv_sem=xr.at[k, inverse(q)],
                device_id=xy_dev(q),
                device_id_type=MESH,
            )
            for q in NEAR
        ]
        for copy in copies:
            start(copy)
        dst[pl.ds(0, 16), cols] = src[pl.ds(0, 16), cols]
        return copies

    def arrive(copies):
        for copy in copies:
            copy.wait_recv()

    ui = iota((128, 128), 0)
    uj = iota((128, 128), 1)

    def pack_rows(src):
        x3[...] = jnp.zeros((128, PW), BF)
        for j in range(3):
            x3[pl.ds(16 * j, 16), :] = src[:, PW * j : PW * (j + 1)]
        for j in range(5):
            x3[pl.ds(48 + 16 * j, 16), pl.ds(128 * j, 128)] = src[:, 3 * PW : D]

    def pack_notes(notes):
        for j in range(5):
            x3[pl.ds(48 + 16 * j, 16), pl.ds(128 * (5 + j // 2), 128)] = notes[:, pl.ds(128 * (j % 2), 128)]

    def pack_in(mat, dst, first=0, width=PW):
        cols = pl.ds(first, width)
        dst[:, cols] = jnp.dot(mat[...], x3[:, cols], preferred_element_type=F32).astype(BF)

    tiled = jnp.dot(
        routes_t[...].astype(F32).astype(BF),
        one_hot((iota((16, 128), 1) & 15) == iota((16, 128), 0)),
        preferred_element_type=F32,
    )
    amat[...] = route_matrix(tiled.astype(I32), y, x)
    pack_rows(tok)
    pack_in(amat, pack_t, *PIECES[0])

    raw_i = remote(info, info2, z_dev(2))
    raw_t = remote(tok, tok2, z_dev(2))
    raw_u = remote(ups, ups2, z_dev(2))

    pl.semaphore_wait(barrier, 19)
    sent_t = [xy_send(0, pack_t, got_t, *PIECES[0])]

    seq_w = seq_weight(seq_ids, ratios)
    rw = (combine_t[...] * seq_w).astype(BF).astype(F32)
    info[:, pl.ds(256, 128)] = jnp.concatenate([tiled, jnp.zeros((8, 128), F32)], axis=0).astype(BF)
    expert = iota((128, 16), 0)
    same = one_hot(ui == uj)
    for half in range(2):
        acc = jnp.zeros((128, 16), F32)
        for k in range(8):
            acc = acc + jnp.where(routes_t[k : k + 1, :] == expert - 64 * half, rw[k : k + 1, :], 0.0)
        info[:, pl.ds(128 * half, 128)] = lax.dot_general(
            acc.astype(BF), same, TN, preferred_element_type=F32
        ).astype(BF)
    pack_notes(info)
    pack_in(amat, pack_t, *PIECES[1])
    sent_t.append(xy_send(6, pack_t, got_t, *PIECES[1]))
    start(raw_i)
    start(raw_t)
    start(raw_u)
    pack_rows(ups)
    pack_in(amat, pack_u)
    sent_u = xy_send(1, pack_u, got_u)
    for copy in loads:
        copy.start()

    brow = iota((4 * ROWS, 256), 0)
    part = jnp.where(brow >= 80, 1, 0) + jnp.where(brow >= 160, 1, 0) + jnp.where(brow >= 240, 1, 0)
    rem = brow - 80 * part
    bq = (rem * 205) >> 10
    bs = rem - 5 * bq
    bmat[...] = one_hot(iota((4 * ROWS, 256), 1) == bq * 16 + jnp.where(part < 3, 5 * part + bs, 15))
    drow = iota((ROWS, 128), 0)
    dlane = iota((ROWS, 128), 1)
    ds_ = drow - 5 * ((drow * 205) >> 10)
    take = one_hot(((ui & 63) == 3 * node + uj) & (uj < 3))

    def unpack(p, got, dst, place, notes=False):
        first, width = PIECES[p]
        dense = jnp.dot(bmat[...], got[:, pl.ds(first, width)], preferred_element_type=F32)
        for j in range(3):
            dst[place, pl.ds(PW * j + first, width)] = dense[ROWS * j : ROWS * (j + 1), :].astype(BF)
        last = dense[3 * ROWS : 4 * ROWS, :]
        if p == 0:
            tail = jnp.zeros((ROWS, 128), F32)
            for j in range(5):
                tail = jnp.where(ds_ == j, last[:, 128 * j : 128 * (j + 1)], tail)
            dst[place, pl.ds(3 * PW, 128)] = tail.astype(BF)
        elif notes:
            picked = jnp.zeros((ROWS, 128), F32)
            for j in range(5):
                mine = (ds_ == j) & ((dlane >> 6) == j % 2)
                picked = jnp.where(mine, last[:, 128 * (j // 2) : 128 * (1 + j // 2)], picked)
            dst[place, pl.ds(D, 128)] = jnp.dot(picked.astype(BF), take, preferred_element_type=F32).astype(BF)

    def gather_copy(buf, src, dst, device):
        return remote(buf.at[slot(*src), :], buf.at[slot(*dst), :], device)

    def pieces(src, dst, device):
        return [[remote(src(cols), dst(cols), device) for cols in dense_slices(p)] for p in range(2)]

    tp = pieces(lambda cols: xb.at[slot(0, 0), cols], lambda cols: xb.at[slot(3, 0), cols], z_dev(1))
    tm = pieces(lambda cols: xb.at[slot(0, 0), cols], lambda cols: xb.at[slot(1, 0), cols], z_dev(3))
    def half_copies(src, dst, device):
        return [remote(src(cols), dst(cols), device) for cols in (pl.ds(0, CA), pl.ds(CA, D - CA))]

    up = half_copies(lambda cols: ub.at[slot(0, 0), cols], lambda cols: ub.at[slot(3, 0), cols], z_dev(1))
    um = half_copies(lambda cols: ub.at[slot(0, 0), cols], lambda cols: ub.at[slot(1, 0), cols], z_dev(3))
    t_sib = {dz: gather_copy(xb, (dz, 0), (dz, 1), sib) for dz in range(4)}
    u_sib = {dz: gather_copy(ub, (dz, 0), (dz, 1), sib) for dz in (0, 2)}
    for dz in (1, 3):
        u_sib[dz] = half_copies(
            lambda cols, dz=dz: ub.at[slot(dz, 0), cols], lambda cols, dz=dz: ub.at[slot(dz, 1), cols], sib
        )

    for p in range(2):
        arrive(sent_t[p])
        unpack(p, got_t, xb, slot(0, 0), True)
        for plus, minus in zip(tp[p], tm[p]):
            start(plus)
            start(minus)
    start(t_sib[0])

    raw_i.wait_recv()
    amat2[...] = route_matrix(info2[:, pl.ds(256, 128)].astype(F32).astype(I32), y, x)
    raw_t.wait_recv()
    pack_rows(tok2)
    pack_notes(info2)
    pack_in(amat2, pack_t2)
    sent_t2 = xy_send(2, pack_t2, got_t2)
    raw_u.wait_recv()
    pack_rows(ups2)
    pack_in(amat2, pack_u2)
    arrive(sent_u)
    sent_u2 = xy_send(3, pack_u2, got_u2)
    for p in range(2):
        unpack(p, got_u, ub, slot(0, 0))
    for h in range(2):
        start(up[h])
        start(um[h])
    start(u_sib[0])

    def gate_up(r0, m):
        rows = pl.ds(r0, m)
        for e in range(3):
            pre[rows, pl.ds(256 * e, 256)] = jnp.dot(
                xb[rows, pl.ds(0, D)], wall[:, pl.ds(256 * e, 256)], preferred_element_type=F32
            )

    def backward(r0, m, chips):
        rows = pl.ds(r0, m)
        proj_all = lax.dot_general(ub[rows, :], wdn[...], NT, preferred_element_type=F32)
        score = jnp.zeros((m, 128), F32)
        lanes = iota((m, 128), 1)
        for e in range(3):
            gate = pre[rows, pl.ds(256 * e, 128)]
            upv = pre[rows, pl.ds(256 * e + 128, 128)]
            proj = proj_all[:, 128 * e : 128 * (e + 1)]
            scale = xb[rows, pl.ds(D, 128)][:, e : e + 1].astype(F32)
            sig = jax.nn.sigmoid(gate)
            act = gate * sig
            hidden = (act * upv).astype(BF).astype(F32)
            score = jnp.where(lanes == e, jnp.sum(hidden * proj, axis=1, keepdims=True), score)
            dh = scale * proj
            dall[rows, pl.ds(256 * e, 128)] = (dh * upv * sig * (1.0 + gate * (1.0 - sig))).astype(BF)
            dall[rows, pl.ds(256 * e + 128, 128)] = (dh * act).astype(BF)
            scl[rows, pl.ds(128 * e, 128)] = (hidden * scale).astype(BF)
        pb[rows, pl.ds(D, 128)] = score.astype(BF)

        def partial(first, last):
            for i in range(first, last):
                cols = pl.ds(512 * i, 512)
                pb[rows, cols] = lax.dot_general(
                    dall[rows, :], wall[cols, :], NT, preferred_element_type=F32
                ).astype(BF)

        partial(0, 4)
        for dz in chips:
            start(p_sib[dz][0])
        partial(4, 7)
        for dz in chips:
            start(p_sib[dz][1])

    p_sib = {
        dz: [
            remote(pb.at[slot(dz, 1), cols], sb.at[pl.ds(POS[dz] * ROWS, ROWS), cols], sib)
            for cols in (pl.ds(0, 2048), pl.ds(2048, DT - 2048))
        ]
        for dz in range(4)
    }

    def pair_sum(dz, cols):
        return pb[slot(dz, 0), cols].astype(F32) + sb[pl.ds(POS[dz] * ROWS, ROWS), cols].astype(F32)

    crow = iota((256, 384), 0)
    clane = iota((256, 384), 1)
    cpart = jnp.where(clane >= 80, 1, 0) + jnp.where(clane >= 160, 1, 0) + jnp.where(clane >= 240, 1, 0)
    crem = clane - 80 * cpart
    cq = (crem * 205) >> 10
    cs = crem - 5 * cq
    cmat[...] = one_hot((crow == cq * 16 + jnp.where(cpart < 3, 5 * cpart + cs, 15)) & (clane < 320))
    x4[...] = jnp.zeros((384, PW), BF)
    repeat = one_hot((ui == (uj & 7)) & (ui < 3))

    def pack_out(p, total, dst):
        first, width = PIECES[p]
        slices = dense_slices(p)
        for j in range(3):
            x4[pl.ds(ROWS * j, ROWS), pl.ds(first, width)] = total(slices[j]).astype(BF)
        extra = total(slices[3])
        if p == 0:
            for j in range(5):
                x4[pl.ds(3 * ROWS, ROWS), pl.ds(128 * j, 128)] = jnp.where(ds_ == j, extra, 0.0).astype(BF)
        else:
            score = jnp.dot(extra.astype(BF), repeat, preferred_element_type=F32)
            x4[pl.ds(3 * ROWS, ROWS), pl.ds(640, 128)] = jnp.where((dlane >> 3) == ds_, score, 0.0).astype(BF)
        dst[:, pl.ds(first, width)] = jnp.dot(
            cmat[...], x4[:, pl.ds(first, width)], preferred_element_type=F32
        ).astype(BF)

    for copy in loads:
        copy.wait()
    t_sib[0].wait_recv()
    gate_up(0, 160)

    arrive(tp[0] + tp[1])
    start(t_sib[3])
    arrive(tm[0] + tm[1])
    start(t_sib[1])
    arrive(sent_t2)
    for p in range(2):
        unpack(p, got_t2, xb, slot(2, 0), True)
    start(t_sib[2])
    t_sib[1].wait_recv()
    t_sib[3].wait_recv()
    gate_up(160, 320)
    t_sib[2].wait_recv()
    gate_up(480, 160)
    arrive(sent_u2)
    for p in range(2):
        unpack(p, got_u2, ub, slot(2, 0))
    start(u_sib[2])
    for h in range(2):
        um[h].wait_recv()
        start(u_sib[1][h])
        up[h].wait_recv()
        start(u_sib[3][h])
    u_sib[2].wait_recv()
    backward(480, 160, (2,))
    arrive(u_sib[1] + u_sib[3])
    backward(160, 320, (1, 3))
    r1 = pieces(lambda cols: pb.at[slot(1, 0), cols], lambda cols: fin.at[0, :, cols], z_dev(1))
    r3 = pieces(lambda cols: pb.at[slot(3, 0), cols], lambda cols: fin.at[1, :, cols], z_dev(3))

    def reduce_send(p):
        for dz, copies in ((1, r1), (3, r3)):
            for cols, copy in zip(dense_slices(p), copies[p]):
                pb[slot(dz, 0), cols] = pair_sum(dz, cols).astype(BF)
                start(copy)

    arrive(p_sib[1] + p_sib[3])
    reduce_send(0)
    arrive(p_sib[2])
    for p in range(2):
        pack_out(p, lambda cols: pair_sum(2, cols), pack_b2)
    sent_b2 = xy_send(4, pack_b2, got_b2)

    def weight_grads(first, last):
        @pl.loop(first, last)
        def _(i):
            cols = pl.ds(pl.multiple_of(i * 512, 512), 512)
            grads = lax.dot_general(xb[:, cols], dall[...], TN, preferred_element_type=F32).astype(BF)
            for e in range(3):
                gg[e, cols, :] = grads[:, 256 * e : 256 * e + 128]
                gu[e, cols, :] = grads[:, 256 * e + 128 : 256 * (e + 1)]

    def down_grads(first, last):
        @pl.loop(first, last)
        def _(i):
            cols = pl.ds(pl.multiple_of(i * 512, 512), 512)
            grads = lax.dot_general(scl[...], ub[:, cols], TN, preferred_element_type=F32).astype(BF)
            for e in range(3):
                gd[e, :, cols] = grads[128 * e : 128 * (e + 1), :]

    u_sib[0].wait_recv()
    backward(0, 160, (0,))
    weight_grads(0, 1)
    reduce_send(1)
    weight_grads(1, 2)
    weight_grads(2, 5)
    arrive(sent_b2)
    parts, tail, score = token_sums(amat2, got_b2, y, x)
    for j in range(3):
        far_out[:, pl.ds(PW * j, PW)] = parts[j].astype(BF)
    far_out[:, pl.ds(3 * PW, 128)] = tail.astype(BF)
    far_out[:, pl.ds(D, 128)] = score.astype(BF)
    raw_b = remote(far_out, far, z_dev(2))
    start(raw_b)
    arrive(p_sib[0])
    sent_b = []
    for p in range(2):
        arrive(r1[p] + r3[p])
        pack_out(
            p, lambda cols: pair_sum(0, cols) + fin[0, :, cols].astype(F32) + fin[1, :, cols].astype(F32), pack_b
        )
        sent_b.append(xy_send(5 + 2 * p, pack_b, got_b, *PIECES[p]))
        if p == 0:
            weight_grads(5, 7)
    down_grads(0, 7)
    raw_b.wait_recv()
    for p in range(2):
        arrive(sent_b[p])
    for copy in started:
        copy.wait_send()


def finish(amat, got_b, far, routes_t, seq_ids, ratios, gg_in, gu_in, gd_in, gt, gc, gg, gu, gd, sems):
    copies = []
    for k, (src, dst) in enumerate(((gg_in, gg), (gu_in, gu), (gd_in, gd))):
        for e in range(3):
            copies.append(pltpu.make_async_copy(src.at[e], dst.at[e], sems.at[3 * k + e]))
    for copy in copies:
        copy.start()
    node = lax.axis_index("node")
    seq_w = seq_weight(seq_ids, ratios)
    parts, tail, score = token_sums(amat, got_b, node // 4, node % 4)
    for j in range(3):
        gt[:, pl.ds(PW * j, PW)] = (parts[j] + far[:, pl.ds(PW * j, PW)].astype(F32)).astype(BF)
    gt[:, pl.ds(3 * PW, 128)] = (tail + far[:, pl.ds(3 * PW, 128)].astype(F32)).astype(BF)
    score = score + far[:, pl.ds(D, 128)].astype(F32)
    eye = one_hot(iota((16, 16), 0) == iota((16, 16), 1))
    scores = lax.dot_general(score.astype(BF), eye, TN, preferred_element_type=F32)
    expert = iota((128, 16), 0)
    for k in range(8):
        value = jnp.sum(jnp.where(routes_t[k : k + 1, :] == expert, scores, 0.0), axis=0, keepdims=True)
        gc[pl.ds(k, 1), :] = value * seq_w[k : k + 1, :]
    for copy in copies:
        copy.wait()


def local(tokens, upstream, routes, combine, seq_ids, ratios, w_gate, w_up, w_down):
    vmem = pl.BlockSpec(memory_space=pltpu.VMEM)
    hbm = pl.BlockSpec(memory_space=pl.ANY)
    shape = jax.ShapeDtypeStruct
    dma = pltpu.SemaphoreType.DMA
    routes_t, combine_t, seq_ids, ratios = routes.T, combine.T, seq_ids[None, :], ratios[None, :]
    amat, got_b, far, *grads = pl.pallas_call(
        kernel,
        out_shape=(
            pltpu.VMEM((256, 128), BF),
            pltpu.VMEM((256, PW), BF),
            pltpu.VMEM((16, DT), BF),
            pltpu.VMEM((3, D, 128), BF),
            pltpu.VMEM((3, D, 128), BF),
            pltpu.VMEM((3, 128, D), BF),
        ),
        in_specs=[vmem] * 6 + [hbm] * 3,
        out_specs=(vmem,) * 6,
        scratch_shapes=[
            pltpu.VMEM((256, 128), BF),
            pltpu.VMEM((320, 256), BF),
            pltpu.VMEM((256, 384), BF),
            pltpu.VMEM((128, PW), BF),
            pltpu.VMEM((16, 384), BF),
            pltpu.VMEM((16, D), BF),
            pltpu.VMEM((16, D), BF),
            pltpu.VMEM((16, 384), BF),
            pltpu.VMEM((16, DT), BF),
        ]
        + [pltpu.VMEM((256, PW), BF)] * 11
        + [
            pltpu.VMEM((640, DT), BF),
            pltpu.VMEM((640, D), BF),
            pltpu.VMEM((D, 768), BF),
            pltpu.VMEM((384, D), BF),
            pltpu.VMEM((640, 768), F32),
            pltpu.VMEM((640, 768), BF),
            pltpu.VMEM((640, 384), BF),
            pltpu.VMEM((640, DT), BF),
            pltpu.VMEM((320, DT), BF),
            pltpu.VMEM((2, ROWS, DT), BF),
            pltpu.VMEM((384, PW), BF),
            dma((9,)), dma((8, 16)), dma((8, 16)), dma((64,)), dma((64,)),
        ],
        compiler_params=pltpu.CompilerParams(
            collective_id=0, has_side_effects=True, vmem_limit_bytes=46 << 20
        ),
        name="moe_grad",
    )(tokens, upstream, routes_t, combine_t, seq_ids, ratios, w_gate, w_up, w_down)
    gt, gc, gg, gu, gd = pl.pallas_call(
        finish,
        out_shape=(
            shape((16, D), BF),
            shape((8, 16), F32),
            shape((3, D, 128), BF),
            shape((3, D, 128), BF),
            shape((3, 128, D), BF),
        ),
        in_specs=[vmem] * 9,
        out_specs=(vmem, vmem, hbm, hbm, hbm),
        scratch_shapes=[dma((9,))],
        compiler_params=pltpu.CompilerParams(vmem_limit_bytes=16 << 20),
        name="moe_finish",
    )(amat, got_b, far, routes_t, seq_ids, ratios, *grads)
    return gt, gc.T, gg, gu, gd


def solution(mesh):
    rows = P(("node", "local"), None)
    return jax.shard_map(
        local,
        mesh=mesh,
        in_specs=(
            rows, rows, rows, rows, P(("node", "local")), P(),
            P("node", None, "local"), P("node", None, "local"), P("node", "local", None),
        ),
        out_specs=(rows, rows, P("node", None, "local"), P("node", None, "local"), P("node", "local", None)),
        check_vma=False,
    )
```
